256 devices in a mesh: cfg: 2 (over core), blk: 16 (over z_hi, y), uly: 8 (over x, z_lo).
Axes of the slice: x: 4, y: 4, z: 8 (z_hi: 4, z_lo: 2; z = z_hi * 2 + z_lo), core: 2. Of those that a mesh axis runs over, the one named last changes fastest.
Arguments:
- hidden: bfloat16 [2, 10240, 2432], P('cfg', ('blk', 'uly')), may hold values from -6 to 6
- text_states: bfloat16 [2, 336, 2432], P('cfg', 'blk'), may hold values from -72 to 72
- modulation: float32 [2, 5, 2432], P('cfg'), may hold values from -3 to 3
- w_qkv: bfloat16 [3, 2432, 2048], P(None, None, 'uly'), may hold values from -0.125 to 0.125
- w_text: bfloat16 [2, 2432, 2048], P(None, None, 'uly'), may hold values from -0.125 to 0.125
- w_out: bfloat16 [2048, 2432], P('uly'), may hold values from -0.125 to 0.125
- qk_gain: float32 [2, 64], replicated, may hold values from 0.8 to 5
- w_final: bfloat16 [2432, 64], replicated, may hold values from -0.125 to 0.125
- w_patch: bfloat16 [64, 2432], replicated, may hold values from -0.75 to 0.75
- position: bfloat16 [10240, 2432], P(('blk', 'uly'), 'cfg'), may hold values from -6 to 6
- latent: float32 [10240, 64], P(('blk', 'uly')), may hold values from -6 to 6
- text_len: int32 [2], P('cfg'), may hold values from 84 to 336, as said below
- timestep: int32 [1], replicated, may hold values from 0 to 27
- sigma_table: int32 [29], replicated, may hold values from 0 to 1000, as said below
Outputs:
- guided: float32 [10240, 64], P(('blk', 'uly'), 'cfg')
- next_latent: float32 [10240, 64], P(('blk', 'uly'), 'cfg')
- next_hidden: bfloat16 [10240, 2432], P(('blk', 'uly'), 'cfg')
The draws below stay inside these ranges and needn't reach their ends.
Inputs may be any that keep to these rules, and one draw needn't show every extreme that they name: `text_len`: entry 1 equals 336; entry 0 is at least 84. `sigma_table`: non-increasing, 1000 at index 0 and 0 at index 28.
All inputs are finite; a program needn't handle non-finite values.
Results may differ from the reference program's by a relative error of at most 0.012.
The reference program's roundings to bfloat16 on the way (of `modulated`, `values`, `attended` and `final`) count: a program that leaves them out, or rounds other values in their place, can miss the bound.
Values may be sent and summed in bfloat16 or wider, within the bound.
A program may use at most 128 MiB of HBM per device.

```python
import jax
import jax.numpy as jnp
from jax import lax

D = 2432
HEADS = 32
HEAD = 64
LAT = 64
TXT = 336
STEPS = 28
IMG = 10240
HD = 2048


def draw_qk_gain(key, part):
    key = jax.random.fold_in(key, 11)
    return jax.random.uniform(key, (2, HEAD), jnp.float32, 0.8, 2.0)


def draw_text_len(key, part):
    key = jax.random.fold_in(key, 12)
    first_len = jax.random.randint(key, (1,), TXT // 4, TXT + 1)
    return jnp.concatenate([first_len, jnp.full((1,), TXT, jnp.int32)]).astype(jnp.int32)


def draw_sigma_table(key, part):
    key = jax.random.fold_in(key, 13)
    decrements = jax.random.randint(key, (STEPS,), 20, 61)
    levels = jnp.maximum(1000 - jnp.cumsum(decrements), 0)
    table = jnp.concatenate([jnp.full((1,), 1000, jnp.int32), levels.astype(jnp.int32)])
    return table.at[STEPS].set(0).astype(jnp.int32)


def block_levels(key, dims, shards, least, top_value):
    level = 1.0
    for dim, shards_of in shards:
        steps = jax.random.uniform(jax.random.fold_in(jax.random.fold_in(key, 6), dim), (shards_of,), jnp.float32, least / len(shards), top_value / len(shards))
        level = level * jnp.repeat(jnp.exp(steps), dims[dim] // shards_of).reshape((-1,) + (1,) * (len(dims) - 1 - dim))
    return level


def bell_draw(rng, shape, deviation, limit, cuts=(), dtype=jnp.bfloat16):
    array = jax.random.normal(rng, shape, jnp.float32) * deviation
    if len(cuts) > 0:
        array = block_levels(rng, shape, cuts, -0.22, 0.18) * array
    return jnp.clip(array, min=-limit, max=limit).astype(dtype)


def setup_inputs(seed: int = 0) -> dict:
    seeds = jax.random.split(jax.random.key(seed), 15)
    hidden = bell_draw(seeds[0], (2, IMG, D), 1.0, 6.0, ((0, 2), (1, 128)))
    text_states = bell_draw(seeds[1], (2, TXT, D), 12.0, 72.0, ((0, 2), (1, 16)))
    modulation = bell_draw(seeds[2], (2, 5, D), 0.5, 3.0, ((0, 2),), jnp.float32)
    w_qkv = bell_draw(seeds[3], (3, D, HD), D ** -0.5, 0.125, ((2, 8),))
    w_text = bell_draw(seeds[4], (2, D, HD), D ** -0.5, 0.125, ((2, 8),))
    w_out = bell_draw(seeds[5], (HD, D), HD ** -0.5, 0.125, ((0, 8),))
    qk_gain = draw_qk_gain(jax.random.fold_in(seeds[14], 71), 0)
    w_final = bell_draw(seeds[7], (D, LAT), D ** -0.5, 0.125)
    w_patch = bell_draw(seeds[8], (LAT, D), LAT ** -0.5, 0.75)
    position = bell_draw(seeds[9], (IMG, D), 1.0, 6.0, ((0, 128), (1, 2)))
    latent = bell_draw(seeds[10], (IMG, LAT), 1.0, 6.0, ((0, 128),), jnp.float32)
    text_len = draw_text_len(jax.random.fold_in(seeds[14], 71), 0)
    timestep = jax.random.randint(seeds[12], (1,), 0, STEPS).astype(jnp.int32)
    sigma_table = draw_sigma_table(jax.random.fold_in(seeds[14], 71), 0)
    return dict(hidden=hidden, text_states=text_states, modulation=modulation, w_qkv=w_qkv, w_text=w_text, w_out=w_out, qk_gain=qk_gain, w_final=w_final, w_patch=w_patch, position=position, latent=latent, text_len=text_len, timestep=timestep, sigma_table=sigma_table)


guidance = 3.5
epsilon = 1e-06

def layer_norm(values):
    average = lax.optimization_barrier(jnp.mean(values, axis=-1, keepdims=True))
    centered = values - average
    spread = lax.optimization_barrier(jnp.mean(centered * centered, axis=-1, keepdims=True))
    return centered * lax.rsqrt(spread + epsilon)

def rms_heads(values, gain):
    row_total = values.shape[0]
    split = values.reshape(row_total, HEADS, HEAD)
    normed = split * lax.rsqrt(lax.optimization_barrier(jnp.mean(split * split, axis=-1, keepdims=True)) + epsilon) * gain
    return normed.reshape(row_total, HEADS * HEAD).astype(jnp.bfloat16)

def one_branch(states, text_rows, modulation, w_qkv, w_text, w_out, qk_gain, w_final, text_count):
    modulated = (layer_norm(states) * (1.0 + modulation[1]) + modulation[0]).astype(jnp.bfloat16)
    queries = rms_heads(jnp.dot(modulated, w_qkv[0], preferred_element_type=jnp.float32), qk_gain[0])
    keys = rms_heads(jnp.dot(modulated, w_qkv[1], preferred_element_type=jnp.float32), qk_gain[1])
    values = jnp.dot(modulated, w_qkv[2], preferred_element_type=jnp.float32).astype(jnp.bfloat16)
    text_keys = rms_heads(jnp.dot(text_rows, w_text[0], preferred_element_type=jnp.float32), qk_gain[1])
    text_values = jnp.dot(text_rows, w_text[1], preferred_element_type=jnp.float32).astype(jnp.bfloat16)
    all_keys = jnp.concatenate([text_keys, keys], axis=0)
    all_values = jnp.concatenate([text_values, values], axis=0)
    usable = jnp.concatenate([jnp.arange(TXT) < text_count, jnp.ones((IMG,), bool)])
    query_heads = queries.reshape(IMG, HEADS, HEAD).transpose(1, 0, 2)
    key_heads = all_keys.reshape(-1, HEADS, HEAD).transpose(1, 0, 2)
    value_heads = all_values.reshape(-1, HEADS, HEAD).transpose(1, 0, 2)

    def attend(operands):
        query_one, key_one, value_one = operands
        scores = jnp.dot(query_one, key_one.T, preferred_element_type=jnp.float32) * HEAD ** (-0.5)
        scores = jnp.where(usable[None, :], scores, -1e+30)
        highest = lax.optimization_barrier(jnp.max(scores, axis=-1, keepdims=True))
        weights = jnp.exp(scores - highest)
        total = lax.optimization_barrier(jnp.sum(weights, axis=-1, keepdims=True))
        summed = jnp.dot(weights.astype(jnp.bfloat16), value_one, preferred_element_type=jnp.float32)
        return (summed / total).astype(jnp.bfloat16)
    attended = lax.map(attend, (query_heads, key_heads, value_heads))
    attended = attended.transpose(1, 0, 2).reshape(IMG, HEADS * HEAD)
    projected = jnp.dot(attended, w_out, preferred_element_type=jnp.float32)
    mixed = states + modulation[2] * projected
    final = (layer_norm(mixed) * (1.0 + modulation[4]) + modulation[3]).astype(jnp.bfloat16)
    return jnp.dot(final, w_final, preferred_element_type=jnp.float32)

def reference(hidden, text_states, modulation, w_qkv, w_text, w_out, qk_gain, w_final, w_patch, position, latent, text_len, timestep, sigma_table):
    velocities = []
    for branch in range(2):
        velocities.append(one_branch(hidden[branch].astype(jnp.float32), text_states[branch], modulation[branch], w_qkv, w_text, w_out, qk_gain, w_final, text_len[branch]))
    guided = velocities[1] + guidance * (velocities[0] - velocities[1])
    sigmas = sigma_table.astype(jnp.float32) / 1000.0
    step_now = timestep[0]
    next_latent = latent + (sigmas[step_now + 1] - sigmas[step_now]) * guided
    embedded = jnp.dot(next_latent.astype(jnp.bfloat16), w_patch, preferred_element_type=jnp.float32)
    next_hidden = (embedded + position.astype(jnp.float32)).astype(jnp.bfloat16)
    return (guided, next_latent, next_hidden)
```

```python
import functools

import jax
import jax.numpy as jnp
import numpy as np
from jax import lax
from jax.experimental import pallas as pl
from jax.experimental.pallas import tpu as pltpu
from jax.sharding import PartitionSpec as P

HEAD = 64
guidance = 3.5
epsilon = 1e-06
MESH = pl.DeviceIdType.MESH
bf16 = jnp.bfloat16
f32 = jnp.float32

ROWS = 80
PAIR = 160
TXT_ROWS = 21
TXT_PAD = 32
FIRST = 48


def layer_norm(values):
    average = jnp.mean(values, axis=-1, keepdims=True)
    centered = values - average
    spread = jnp.mean(centered * centered, axis=-1, keepdims=True)
    return centered * lax.rsqrt(spread + epsilon)


def coords():
    c = lax.axis_index("cfg")
    b = lax.axis_index("blk")
    u = lax.axis_index("uly")
    return c, b // 4, b % 4, u // 2, u % 2


def head_norm(values, gain):
    rows = values.shape[0]
    low = lax.broadcasted_iota(jnp.int32, (rows, 128), 1) < HEAD
    columns = []
    for t in range(2):
        x = values[:, 128 * t : 128 * t + 128]
        sq = x * x
        a = jnp.sum(jnp.where(low, sq, 0.0), axis=1, keepdims=True)
        b = jnp.sum(jnp.where(low, 0.0, sq), axis=1, keepdims=True)
        scale = lax.rsqrt(jnp.where(low, a, b) * (1.0 / HEAD) + epsilon)
        columns.append(x * scale * gain)
    return columns


def pack_heads(left, right):
    rows = left[0].shape[0]
    low = lax.broadcasted_iota(jnp.int32, (rows, 128), 1) < HEAD
    out = []
    for t in range(2):
        out.append(jnp.where(low, left[t], pltpu.roll(right[t], HEAD, 1)))
        out.append(jnp.where(low, pltpu.roll(left[t], HEAD, 1), right[t]))
    return out


def project_kernel(
    hid_ref, txt_ref, mod_ref, wqkv_ref, wtext_ref, gain_ref,
    kv_ref, tkv_ref, q_ref,
    mods, wq, wt, txt, kvst, qst, tst,
    wsem, lsem, bsend, brecv, zsend, zrecv, qsend, qrecv, ysend, yrecv,
    tzsend, tzrecv, tysend, tyrecv,
):
    c, zh, y, x, zl = coords()
    u = x * 2 + zl
    blk = zh * 4 + y

    def at(zh_=None, y_=None, x_=None, zl_=None):
        zz = zh if zh_ is None else lax.rem(zh + zh_, 4)
        yy = y if y_ is None else lax.rem(y + y_, 4)
        xx = x if x_ is None else lax.rem(x + x_, 4)
        ll = zl if zl_ is None else 1 - zl
        return (c, zz * 4 + yy, xx * 2 + ll)

    partner = at(zl_=1)
    up, down = at(x_=1), at(x_=3)

    wcopies = []
    for i in range(3):
        wcopies.append(pltpu.make_async_copy(wqkv_ref.at[i], wq.at[i], wsem.at[i]))
    for i in range(2):
        wcopies.append(pltpu.make_async_copy(wtext_ref.at[i], wt.at[i], wsem.at[3 + i]))
    for w in wcopies[3:] + wcopies[:3]:
        w.start()

    barrier = pltpu.get_barrier_semaphore()
    peers = [partner, up, down] + [at(zh_=d) for d in (1, 2, 3)] + [at(y_=d) for d in (1, 2, 3)]
    for peer in peers:
        pl.semaphore_signal(barrier, inc=1, device_id=peer, device_id_type=MESH)

    states = hid_ref[0].astype(f32)
    modulated = layer_norm(states) * (1.0 + mod_ref[0, 1:2, :]) + mod_ref[0, 0:1, :]
    mods[u] = modulated.astype(bf16)
    txt[...] = jnp.zeros_like(txt)
    txt[0:TXT_ROWS, :] = txt_ref[0]
    pl.semaphore_wait(barrier, len(peers))

    def remote(src, dst, send, recv, to):
        return pltpu.make_async_remote_copy(
            src_ref=src, dst_ref=dst, send_sem=send, recv_sem=recv,
            device_id=to, device_id_type=MESH,
        )

    def shard(i, x_, zl_, part, to):
        s = lax.rem(x + x_, 4) * 2 + (zl if zl_ == 0 else 1 - zl)
        ref = mods.at[s]
        if part == 1:
            ref = mods.at[s, pl.ds(0, FIRST)]
        elif part == 2:
            ref = mods.at[s, pl.ds(FIRST, ROWS - FIRST)]
        return remote(ref, ref, bsend.at[i], brecv.at[i], to)

    sends = {
        0: shard(0, 0, 0, 0, partner),
        1: shard(1, 0, 0, 0, up),
        2: shard(2, 0, 0, 0, down),
        3: shard(3, 0, 1, 0, up),
        4: shard(4, 0, 1, 0, down),
        5: shard(5, 3, 0, 1, up),
        6: shard(6, 1, 0, 2, down),
        7: shard(7, 3, 1, 1, up),
        8: shard(8, 1, 1, 2, down),
    }
    arrive = {
        0: shard(0, 0, 1, 0, partner),
        1: shard(1, 3, 0, 0, up),
        2: shard(2, 1, 0, 0, down),
        3: shard(3, 3, 1, 0, up),
        4: shard(4, 1, 1, 0, down),
        5: shard(5, 2, 0, 1, up),
        6: shard(6, 2, 0, 2, down),
        7: shard(7, 2, 1, 1, up),
        8: shard(8, 2, 1, 2, down),
    }
    for i in (0, 1, 2):
        sends[i].start()

    gain_q = gain_ref[0:1, :]
    gain_k = gain_ref[1:2, :]

    def copy_kv(t, p, d):
        h = lax.rem(zh + d, 4)
        return remote(kvst.at[t, h], kv_ref.at[blk, p], zsend.at[t, d - 1], zrecv.at[t, d - 1], at(zh_=d))

    def copy_q(t, p, d):
        h = lax.rem(zh + d, 4)
        return remote(qst.at[t, h], q_ref.at[zh, p], qsend.at[t, d - 1], qrecv.at[t, d - 1], at(zh_=d))

    def landed_kv(t, p, d):
        slot = kv_ref.at[lax.rem(zh + 4 - d, 4) * 4 + y, p]
        return remote(slot, slot, zsend.at[t, d - 1], zrecv.at[t, d - 1], at(zh_=d))

    def landed_q(t, p, d):
        slot = q_ref.at[lax.rem(zh + 4 - d, 4), p]
        return remote(slot, slot, qsend.at[t, d - 1], qrecv.at[t, d - 1], at(zh_=d))

    def copy_y(t, p, d, e):
        if d == 0:
            src, dst = kvst.at[t, zh], kv_ref.at[blk, p]
        else:
            src = dst = kv_ref.at[lax.rem(zh + 4 - d, 4) * 4 + y, p]
        return remote(src, dst, ysend.at[t, d, e - 1], yrecv.at[t, d, e - 1], at(y_=e))

    def landed_y(t, p, d, e):
        slot = kv_ref.at[lax.rem(zh + 4 - d, 4) * 4 + lax.rem(y + 4 - e, 4), p]
        return remote(slot, slot, ysend.at[t, d, e - 1], yrecv.at[t, d, e - 1], at(y_=e))

    def text_z(d):
        h = lax.rem(zh + d, 4)
        return remote(tst.at[h], tkv_ref.at[blk], tzsend.at[d - 1], tzrecv.at[d - 1], at(zh_=d))

    def text_z_landed(d):
        slot = tkv_ref.at[lax.rem(zh + 4 - d, 4) * 4 + y]
        return remote(slot, slot, tzsend.at[d - 1], tzrecv.at[d - 1], at(zh_=d))

    def text_y(d, e):
        if d == 0:
            src, dst = tst.at[zh], tkv_ref.at[blk]
        else:
            src = dst = tkv_ref.at[lax.rem(zh + 4 - d, 4) * 4 + y]
        return remote(src, dst, tysend.at[d, e - 1], tyrecv.at[d, e - 1], at(y_=e))

    def text_y_landed(d, e):
        slot = tkv_ref.at[lax.rem(zh + 4 - d, 4) * 4 + lax.rem(y + 4 - e, 4)]
        return remote(slot, slot, tysend.at[d, e - 1], tyrecv.at[d, e - 1], at(y_=e))

    for w in wcopies[3:]:
        w.wait()
    rows = txt[...]
    tk = head_norm(jnp.dot(rows, wt[0], preferred_element_type=f32), gain_k)
    tv = jnp.dot(rows, wt[1], preferred_element_type=f32)
    for h, value in enumerate(pack_heads(tk, [tv[:, 0:128], tv[:, 128:256]])):
        tst[h] = value.astype(bf16)
    for d in (1, 2, 3):
        text_z(d).start()
    for e in (1, 2, 3):
        text_y(0, e).start()
    local_text = pltpu.make_async_copy(tst.at[zh], tkv_ref.at[blk], lsem.at[8])
    local_text.start()

    for w in wcopies[:3]:
        w.wait()

    def project(t, x_):
        p = lax.rem(x + x_, 4)
        pair = mods[pl.ds(p * 2, 2)].reshape(PAIR, mods.shape[2])
        qs = head_norm(jnp.dot(pair, wq[0], preferred_element_type=f32), gain_q)
        for h, value in enumerate(pack_heads([v[0:ROWS] for v in qs], [v[ROWS:PAIR] for v in qs])):
            qst[t, h] = value.astype(bf16)
        ks = head_norm(jnp.dot(pair, wq[1], preferred_element_type=f32), gain_k)
        vs = jnp.dot(pair, wq[2], preferred_element_type=f32)
        for h, value in enumerate(pack_heads(ks, [vs[:, 0:128], vs[:, 128:256]])):
            kvst[t, h] = value.astype(bf16)
        for d in (2, 1, 3):
            copy_kv(t, p, d).start()
        for d in (2, 1, 3):
            copy_q(t, p, d).start()
        for e in (2, 1, 3):
            copy_y(t, p, 0, e).start()
        pltpu.make_async_copy(kvst.at[t, zh], kv_ref.at[blk, p], lsem.at[t]).start()
        pltpu.make_async_copy(qst.at[t, zh], q_ref.at[zh, p], lsem.at[4 + t]).start()

    def pass_on(t, x_):
        p = lax.rem(x + x_, 4)
        for d in (1, 3, 2):
            landed_kv(t, p, d).wait_recv()
            for e in (2, 1, 3):
                copy_y(t, p, d, e).start()

    arrive[0].wait_recv()
    sends[3].start()
    sends[4].start()
    arrive[1].wait_recv()
    sends[5].start()
    arrive[2].wait_recv()
    sends[6].start()
    project(0, 0)
    for d in (1, 2, 3):
        text_z_landed(d).wait_recv()
        for e in (1, 2, 3):
            text_y(d, e).start()
    arrive[3].wait_recv()
    sends[7].start()
    arrive[4].wait_recv()
    sends[8].start()
    project(1, 3)
    project(2, 1)
    pass_on(0, 0)
    for i in (5, 6, 7, 8):
        arrive[i].wait_recv()
    project(3, 2)
    pass_on(1, 3)
    pass_on(2, 1)
    pass_on(3, 2)

    for i in range(9):
        sends[i].wait_send()
    local_text.wait()
    for d in (1, 2, 3):
        text_z(d).wait_send()
    for d in range(4):
        for e in (1, 2, 3):
            text_y(d, e).wait_send()
            text_y_landed(d, e).wait_recv()
    for t, x_ in enumerate((0, 3, 1, 2)):
        p = lax.rem(x + x_, 4)
        pltpu.make_async_copy(kvst.at[t, zh], kv_ref.at[blk, p], lsem.at[t]).wait()
        pltpu.make_async_copy(qst.at[t, zh], q_ref.at[zh, p], lsem.at[4 + t]).wait()
        for d in (1, 2, 3):
            copy_kv(t, p, d).wait_send()
            copy_q(t, p, d).wait_send()
            landed_q(t, p, d).wait_recv()
        for d in range(4):
            for e in (1, 2, 3):
                copy_y(t, p, d, e).wait_send()
                landed_y(t, p, d, e).wait_recv()


def project_heads(hidden, text_states, modulation, w_qkv, w_text, gains):
    width = hidden.shape[2]
    vmem = pl.BlockSpec(memory_space=pltpu.VMEM)
    hbm = pl.BlockSpec(memory_space=pl.ANY)
    dma = pltpu.SemaphoreType.DMA
    return pl.pallas_call(
        project_kernel,
        out_shape=[
            jax.ShapeDtypeStruct((16, 4, PAIR, 128), bf16),
            jax.ShapeDtypeStruct((16, TXT_PAD, 128), bf16),
            jax.ShapeDtypeStruct((4, 4, ROWS, 128), bf16),
        ],
        in_specs=[vmem, vmem, vmem, hbm, hbm, vmem],
        out_specs=[hbm, hbm, hbm],
        scratch_shapes=[
            pltpu.VMEM((8, ROWS, width), bf16),
            pltpu.VMEM((3, width, 256), bf16),
            pltpu.VMEM((2, width, 256), bf16),
            pltpu.VMEM((TXT_PAD, width), bf16),
            pltpu.VMEM((4, 4, PAIR, 128), bf16),
            pltpu.VMEM((4, 4, ROWS, 128), bf16),
            pltpu.VMEM((4, TXT_PAD, 128), bf16),
            dma((5,)),
            dma((9,)),
            dma((9,)), dma((9,)),
            dma((4, 3)), dma((4, 3)),
            dma((4, 3)), dma((4, 3)),
            dma((4, 4, 3)), dma((4, 4, 3)),
            dma((3,)), dma((3,)),
            dma((4, 3)), dma((4, 3)),
        ],
        compiler_params=pltpu.CompilerParams(
            collective_id=0, has_side_effects=True, vmem_limit_bytes=40 << 20
        ),
        name="project_heads",
    )(hidden, text_states, modulation, w_qkv, w_text, gains)


KEYS = 2560


def attend_kernel(len_ref, q_ref, kv_ref, tkv_ref, o_ref, q2, v1):
    step = pl.program_id(0)
    image = kv_ref.shape[0]
    text = tkv_ref.shape[0]

    @pl.when(step == 0)
    def _():
        def values_and_ones(block):
            wide = block.astype(f32)
            lane = lax.broadcasted_iota(jnp.int32, wide.shape, 1)
            return jnp.where(lane < HEAD, pltpu.roll(wide, HEAD, 1), 1.0).astype(bf16)

        @pl.loop(0, image // 512)
        def _(n):
            rows = pl.ds(pl.multiple_of(n * 512, 512), 512)
            v1[rows, :] = values_and_ones(kv_ref[rows, :])

        v1[image : image + text, :] = values_and_ones(tkv_ref[...])

    low = lax.broadcasted_iota(jnp.int32, (ROWS, 128), 1) < HEAD
    for p in range(4):
        packed = q_ref[0, p].astype(f32)
        q2[PAIR * p : PAIR * p + ROWS, :] = jnp.where(low, packed, 0.0).astype(bf16)
        q2[PAIR * p + ROWS : PAIR * p + PAIR, :] = jnp.where(
            low, pltpu.roll(packed, HEAD, 1), 0.0
        ).astype(bf16)
    q = q2[...]

    def fold(carry, keys, values, usable):
        top, acc = carry
        scores = lax.dot_general(q, keys, (((1,), (1,)), ((), ())), preferred_element_type=f32)
        if usable is not None:
            scores = jnp.where(usable, scores, -1e30)
        new_top = jnp.maximum(top, jnp.max(scores, axis=1, keepdims=True))
        weights = jnp.exp2(scores - new_top).astype(bf16)
        shrink = jnp.exp2(top - new_top)
        return new_top, acc * shrink + jnp.dot(weights, values, preferred_element_type=f32)

    count = q.shape[0]
    carry = (jnp.full((count, 1), -1e30, f32), jnp.zeros((count, 128), f32))

    def image_step(j, carry):
        rows = pl.ds(pl.multiple_of(j * KEYS, KEYS), KEYS)
        return fold(carry, kv_ref[rows, :], v1[rows, :], None)

    carry = lax.fori_loop(0, image // KEYS, image_step, carry)
    row = lax.broadcasted_iota(jnp.int32, (1, text), 1)
    block = row // TXT_PAD
    within = row - block * TXT_PAD
    usable = jnp.logical_and(within < TXT_ROWS, block * TXT_ROWS + within < len_ref[0])
    top, acc = fold(carry, tkv_ref[...], v1[image : image + text, :], usable)
    out = acc / acc[:, HEAD : HEAD + 1]
    high = pltpu.roll(out, HEAD, 1)
    low = lax.broadcasted_iota(jnp.int32, (FIRST, 128), 1) < HEAD
    for s in range(8):
        o_ref[0, s] = jnp.where(
            low,
            out[ROWS * s : ROWS * s + FIRST],
            high[ROWS * (s + 1) - FIRST : ROWS * (s + 1)],
        ).astype(bf16)


def attend(text_len, q, kv, tkv):
    image, text = kv.shape[0], tkv.shape[0]
    return pl.pallas_call(
        attend_kernel,
        grid=(4,),
        in_specs=[
            pl.BlockSpec(memory_space=pltpu.SMEM),
            pl.BlockSpec((1, 4, ROWS, 128), lambda i: (i, 0, 0, 0)),
            pl.BlockSpec((image, 128), lambda i: (0, 0)),
            pl.BlockSpec((text, 128), lambda i: (0, 0)),
        ],
        out_specs=pl.BlockSpec((1, 8, FIRST, 128), lambda i: (i, 0, 0, 0)),
        out_shape=jax.ShapeDtypeStruct((4, 8, FIRST, 128), bf16),
        scratch_shapes=[
            pltpu.VMEM((4 * PAIR, 128), bf16),
            pltpu.VMEM((image + text, 128), bf16),
        ],
        compiler_params=pltpu.CompilerParams(vmem_limit_bytes=44 << 20),
        cost_estimate=pl.CostEstimate(
            flops=4 * 4 * 4 * PAIR * (image + text) * 128,
            bytes_accessed=3 * image * 128 * 2,
            transcendentals=4 * 4 * PAIR * (image + text),
        ),
        name="attend",
    )(text_len, q, kv, tkv)


def finish_kernel(
    o_ref, hid_ref, mod_ref, wout_ref, wfinal_ref, wpatch_ref, pos_ref, lat_ref, time_ref, sigma_ref,
    guided_ref, latent_ref, next_ref,
    got, att, wo, vel, wsem, lsem, osend, orecv, vsend, vrecv,
):
    c, zh, y, x, zl = coords()
    u = x * 2 + zl
    load = pltpu.make_async_copy(wout_ref, wo, wsem.at[0])
    load.start()

    barrier = pltpu.get_barrier_semaphore()
    peers = []
    for k in range(1, 32):
        dz, du = k // 8, k % 8
        peers.append((c, lax.rem(zh + dz, 4) * 4 + y, lax.rem(u + du, 8)))
    other = (1 - c, zh * 4 + y, u)
    for peer in peers + [other]:
        pl.semaphore_signal(barrier, inc=1, device_id=peer, device_id_type=MESH)
    pl.semaphore_wait(barrier, len(peers) + 1)

    def remote(src, dst, send, recv, to):
        return pltpu.make_async_remote_copy(
            src_ref=src, dst_ref=dst, send_sem=send, recv_sem=recv,
            device_id=to, device_id_type=MESH,
        )

    def out_copy(k):
        dz, du = k // 8, k % 8
        z2, u2 = lax.rem(zh + dz, 4), lax.rem(u + du, 8)
        return remote(
            o_ref.at[z2, u2], got.at[u, zh], osend.at[k], orecv.at[k], peers[k - 1]
        )

    def in_copy(k):
        dz, du = k // 8, k % 8
        z2, u2 = lax.rem(zh + 4 - dz, 4), lax.rem(u + 8 - du, 8)
        slot = got.at[u2, z2]
        return remote(slot, slot, osend.at[k], orecv.at[k], peers[k - 1])

    for k in range(31, 0, -1):
        out_copy(k).start()
    own = pltpu.make_async_copy(o_ref.at[zh, u], got.at[u, zh], lsem.at[0])
    own.start()

    states = hid_ref[0].astype(f32)
    is_cond = c == 0
    half = pos_ref.shape[1]
    patch = wpatch_ref[...].astype(f32)
    patch = jnp.where(is_cond, patch[:, 0:half], patch[:, half : 2 * half]).astype(bf16)
    t = time_ref[0]
    sigma_now = sigma_ref[t].astype(f32) / 1000.0
    sigma_next = sigma_ref[t + 1].astype(f32) / 1000.0

    own.wait()
    for k in range(1, 32):
        in_copy(k).wait_recv()
    low = lax.broadcasted_iota(jnp.int32, (FIRST, 128), 1) < HEAD
    for s in range(8):
        for pair in range(2):
            even = got[s, 2 * pair].astype(f32)
            odd = got[s, 2 * pair + 1].astype(f32)
            columns = pl.ds(s * 256 + pair * 128, 128)
            att[0:FIRST, columns] = jnp.where(low, even, pltpu.roll(odd, HEAD, 1)).astype(bf16)
            rest = jnp.where(low, pltpu.roll(even, HEAD, 1), odd).astype(bf16)
            att[FIRST:ROWS, columns] = rest[2 * FIRST - ROWS : FIRST]
    load.wait()
    projected = jnp.dot(att[...], wo[...], preferred_element_type=f32)
    mixed = states + mod_ref[0, 2:3, :] * projected
    final = (layer_norm(mixed) * (1.0 + mod_ref[0, 4:5, :]) + mod_ref[0, 3:4, :]).astype(bf16)
    velocity = jnp.dot(final, wfinal_ref[...], preferred_element_type=f32)
    vel[0] = velocity
    exchange = remote(vel.at[0], vel.at[1], vsend.at[0], vrecv.at[0], other)
    exchange.start()
    exchange.wait()
    partner = vel[1]
    cond = jnp.where(is_cond, velocity, partner)
    uncond = jnp.where(is_cond, partner, velocity)
    guided = uncond + guidance * (cond - uncond)
    latent = lat_ref[...] + (sigma_next - sigma_now) * guided
    embedded = jnp.dot(latent.astype(bf16), patch, preferred_element_type=f32)
    next_ref[...] = (embedded + pos_ref[...].astype(f32)).astype(bf16)
    channels = guided_ref.shape[1]
    guided_ref[...] = jnp.where(is_cond, guided[:, 0:channels], guided[:, channels:])
    latent_ref[...] = jnp.where(is_cond, latent[:, 0:channels], latent[:, channels:])
    for k in range(1, 32):
        out_copy(k).wait_send()


def finish(o, hidden, modulation, whole_out, w_final, w_patch, position, latent, timestep, sigma_table):
    vmem = pl.BlockSpec(memory_space=pltpu.VMEM)
    hbm = pl.BlockSpec(memory_space=pl.ANY)
    smem = pl.BlockSpec(memory_space=pltpu.SMEM)
    dma = pltpu.SemaphoreType.DMA
    channels = latent.shape[1] // 2
    return pl.pallas_call(
        finish_kernel,
        out_shape=[
            jax.ShapeDtypeStruct((ROWS, channels), f32),
            jax.ShapeDtypeStruct((ROWS, channels), f32),
            jax.ShapeDtypeStruct(position.shape, bf16),
        ],
        in_specs=[vmem, vmem, vmem, hbm, vmem, vmem, vmem, vmem, smem, smem],
        out_specs=[vmem, vmem, vmem],
        scratch_shapes=[
            pltpu.VMEM((8, 4, FIRST, 128), bf16),
            pltpu.VMEM((ROWS, whole_out.shape[0]), bf16),
            pltpu.VMEM(whole_out.shape, bf16),
            pltpu.VMEM((2, ROWS, 2 * channels), f32),
            dma((1,)), dma((1,)),
            dma((32,)), dma((32,)),
            dma((1,)), dma((1,)),
        ],
        compiler_params=pltpu.CompilerParams(
            collective_id=1, has_side_effects=True, vmem_limit_bytes=40 << 20
        ),
        name="finish",
    )(o, hidden, modulation, whole_out, w_final, w_patch, position, latent, timestep, sigma_table)


def body(
    hidden, text_states, modulation, w_qkv, w_text, w_out, qk_gain, w_final, w_patch,
    position, latent, text_len, timestep, sigma_table,
):
    scale = np.array([[np.log2(np.e) * HEAD ** -0.5], [1.0]], np.float32)
    gains = jnp.tile(qk_gain * scale, (1, 2))
    kv, tkv, q = project_heads(hidden, text_states, modulation, w_qkv, w_text, gains)
    whole_out = lax.all_gather(w_out, "uly", axis=0, tiled=True)
    o = attend(text_len, q, kv.reshape(-1, 128), tkv.reshape(-1, 128))
    return tuple(
        finish(o, hidden, modulation, whole_out, w_final, w_patch, position, latent, timestep, sigma_table)
    )


def solution(mesh):
    in_specs = (
        P("cfg", ("blk", "uly"), None),
        P("cfg", "blk", None),
        P("cfg", None, None),
        P(None, None, "uly"),
        P(None, None, "uly"),
        P("uly", None),
        P(),
        P(),
        P(),
        P(("blk", "uly"), "cfg"),
        P(("blk", "uly"), None),
        P("cfg"),
        P(),
        P(),
    )
    out_specs = (P(("blk", "uly"), "cfg"), P(("blk", "uly"), "cfg"), P(("blk", "uly"), "cfg"))
    return jax.shard_map(body, mesh=mesh, in_specs=in_specs, out_specs=out_specs, check_vma=False)
```

```python
import functools

import jax
import jax.numpy as jnp
import numpy as np
from jax import lax
from jax.experimental import pallas as pl
from jax.experimental.pallas import tpu as pltpu
from jax.sharding import PartitionSpec as P

HEAD = 64
guidance = 3.5
epsilon = 1e-06
MESH = pl.DeviceIdType.MESH
bf16 = jnp.bfloat16
f32 = jnp.float32

ROWS = 80
PAIR = 160
TXT_ROWS = 21
TXT_PAD = 32
FIRST = 48


def layer_norm(values):
    average = jnp.mean(values, axis=-1, keepdims=True)
    centered = values - average
    spread = jnp.mean(centered * centered, axis=-1, keepdims=True)
    return centered * lax.rsqrt(spread + epsilon)


def coords():
    c = lax.axis_index("cfg")
    b = lax.axis_index("blk")
    u = lax.axis_index("uly")
    return c, b // 4, b % 4, u // 2, u % 2


def head_norm(values, gain):
    rows = values.shape[0]
    low = lax.broadcasted_iota(jnp.int32, (rows, 128), 1) < HEAD
    columns = []
    for t in range(2):
        x = values[:, 128 * t : 128 * t + 128]
        sq = x * x
        a = jnp.sum(jnp.where(low, sq, 0.0), axis=1, keepdims=True)
        b = jnp.sum(jnp.where(low, 0.0, sq), axis=1, keepdims=True)
        scale = lax.rsqrt(jnp.where(low, a, b) * (1.0 / HEAD) + epsilon)
        columns.append(x * scale * gain)
    return columns


def pack_heads(left, right):
    rows = left[0].shape[0]
    low = lax.broadcasted_iota(jnp.int32, (rows, 128), 1) < HEAD
    out = []
    for t in range(2):
        out.append(jnp.where(low, left[t], pltpu.roll(right[t], HEAD, 1)))
        out.append(jnp.where(low, pltpu.roll(left[t], HEAD, 1), right[t]))
    return out


def project_kernel(
    hid_ref, txt_ref, mod_ref, wqkv_ref, wtext_ref, wout_ref, gain_ref,
    kv_ref, tkv_ref, q_ref, wx_ref,
    mods, wq, wt, txt, kvst, qst, tst,
    wsem, lsem, bsend, brecv, zsend, zrecv, qsend, qrecv, ysend, yrecv,
    tzsend, tzrecv, tysend, tyrecv, osend, orecv,
):
    c, zh, y, x, zl = coords()
    u = x * 2 + zl
    blk = zh * 4 + y

    def at(zh_=None, y_=None, x_=None, zl_=None):
        zz = zh if zh_ is None else lax.rem(zh + zh_, 4)
        yy = y if y_ is None else lax.rem(y + y_, 4)
        xx = x if x_ is None else lax.rem(x + x_, 4)
        ll = zl if zl_ is None else 1 - zl
        return (c, zz * 4 + yy, xx * 2 + ll)

    partner = at(zl_=1)
    up, down = at(x_=1), at(x_=3)

    wcopies = []
    for i in range(3):
        wcopies.append(pltpu.make_async_copy(wqkv_ref.at[i], wq.at[i], wsem.at[i]))
    for i in range(2):
        wcopies.append(pltpu.make_async_copy(wtext_ref.at[i], wt.at[i], wsem.at[3 + i]))
    for w in wcopies[3:] + wcopies[:3]:
        w.start()

    barrier = pltpu.get_barrier_semaphore()
    peers = [partner, up, down, at(x_=2)] + [at(zh_=d) for d in (1, 2, 3)] + [at(y_=d) for d in (1, 2, 3)]
    for peer in peers:
        pl.semaphore_signal(barrier, inc=1, device_id=peer, device_id_type=MESH)

    states = hid_ref[0].astype(f32)
    modulated = layer_norm(states) * (1.0 + mod_ref[1]) + mod_ref[0]
    mods[u] = modulated.astype(bf16)
    txt[...] = jnp.zeros_like(txt)
    txt[0:TXT_ROWS, :] = txt_ref[0]
    pl.semaphore_wait(barrier, len(peers))

    def remote(src, dst, send, recv, to):
        return pltpu.make_async_remote_copy(
            src_ref=src, dst_ref=dst, send_sem=send, recv_sem=recv,
            device_id=to, device_id_type=MESH,
        )

    def shard(i, x_, zl_, part, to):
        s = lax.rem(x + x_, 4) * 2 + (zl if zl_ == 0 else 1 - zl)
        ref = mods.at[s]
        if part == 1:
            ref = mods.at[s, pl.ds(0, FIRST)]
        elif part == 2:
            ref = mods.at[s, pl.ds(FIRST, ROWS - FIRST)]
        return remote(ref, ref, bsend.at[i], brecv.at[i], to)

    sends = {
        0: shard(0, 0, 0, 0, partner),
        1: shard(1, 0, 0, 0, up),
        2: shard(2, 0, 0, 0, down),
        3: shard(3, 0, 1, 0, up),
        4: shard(4, 0, 1, 0, down),
        5: shard(5, 3, 0, 1, up),
        6: shard(6, 1, 0, 2, down),
        7: shard(7, 3, 1, 1, up),
        8: shard(8, 1, 1, 2, down),
    }
    arrive = {
        0: shard(0, 0, 1, 0, partner),
        1: shard(1, 3, 0, 0, up),
        2: shard(2, 1, 0, 0, down),
        3: shard(3, 3, 1, 0, up),
        4: shard(4, 1, 1, 0, down),
        5: shard(5, 2, 0, 1, up),
        6: shard(6, 2, 0, 2, down),
        7: shard(7, 2, 1, 1, up),
        8: shard(8, 2, 1, 2, down),
    }
    for i in (0, 1, 2):
        sends[i].start()

    gain_q = gain_ref[0:1, :] * float(np.log2(np.e) * HEAD ** -0.5)
    gain_k = gain_ref[1:2, :]
    gain_q = jnp.concatenate([gain_q, gain_q], axis=1)
    gain_k = jnp.concatenate([gain_k, gain_k], axis=1)
    own_half = wout_ref.at[pl.ds(pl.multiple_of(c * 128, 128), 128)]
    own_out = pltpu.make_async_copy(own_half, wx_ref.at[x], lsem.at[9])
    own_out.start()

    def out_x(d):
        return remote(own_half, wx_ref.at[x], osend.at[d - 1], orecv.at[d - 1], at(x_=d))

    def out_x_landed(d):
        slot = wx_ref.at[lax.rem(x + 4 - d, 4)]
        return remote(slot, slot, osend.at[d - 1], orecv.at[d - 1], at(x_=d))

    def copy_kv(t, p, d):
        h = lax.rem(zh + d, 4)
        return remote(kvst.at[t, h], kv_ref.at[blk, p], zsend.at[t, d - 1], zrecv.at[t, d - 1], at(zh_=d))

    def copy_q(t, p, d):
        h = lax.rem(zh + d, 4)
        return remote(qst.at[t, h], q_ref.at[zh, p], qsend.at[t, d - 1], qrecv.at[t, d - 1], at(zh_=d))

    def landed_kv(t, p, d):
        slot = kv_ref.at[lax.rem(zh + 4 - d, 4) * 4 + y, p]
        return remote(slot, slot, zsend.at[t, d - 1], zrecv.at[t, d - 1], at(zh_=d))

    def landed_q(t, p, d):
        slot = q_ref.at[lax.rem(zh + 4 - d, 4), p]
        return remote(slot, slot, qsend.at[t, d - 1], qrecv.at[t, d - 1], at(zh_=d))

    def copy_y(t, p, d, e):
        if d == 0:
            src, dst = kvst.at[t, zh], kv_ref.at[blk, p]
        else:
            src = dst = kv_ref.at[lax.rem(zh + 4 - d, 4) * 4 + y, p]
        return remote(src, dst, ysend.at[t, d, e - 1], yrecv.at[t, d, e - 1], at(y_=e))

    def landed_y(t, p, d, e):
        slot = kv_ref.at[lax.rem(zh + 4 - d, 4) * 4 + lax.rem(y + 4 - e, 4), p]
        return remote(slot, slot, ysend.at[t, d, e - 1], yrecv.at[t, d, e - 1], at(y_=e))

    def text_z(d):
        h = lax.rem(zh + d, 4)
        return remote(tst.at[h], tkv_ref.at[blk], tzsend.at[d - 1], tzrecv.at[d - 1], at(zh_=d))

    def text_z_landed(d):
        slot = tkv_ref.at[lax.rem(zh + 4 - d, 4) * 4 + y]
        return remote(slot, slot, tzsend.at[d - 1], tzrecv.at[d - 1], at(zh_=d))

    def text_y(d, e):
        if d == 0:
            src, dst = tst.at[zh], tkv_ref.at[blk]
        else:
            src = dst = tkv_ref.at[lax.rem(zh + 4 - d, 4) * 4 + y]
        return remote(src, dst, tysend.at[d, e - 1], tyrecv.at[d, e - 1], at(y_=e))

    def text_y_landed(d, e):
        slot = tkv_ref.at[lax.rem(zh + 4 - d, 4) * 4 + lax.rem(y + 4 - e, 4)]
        return remote(slot, slot, tysend.at[d, e - 1], tyrecv.at[d, e - 1], at(y_=e))

    for w in wcopies[3:]:
        w.wait()
    rows = txt[...]
    tk = head_norm(jnp.dot(rows, wt[0], preferred_element_type=f32), gain_k)
    tv = jnp.dot(rows, wt[1], preferred_element_type=f32)
    for h, value in enumerate(pack_heads(tk, [tv[:, 0:128], tv[:, 128:256]])):
        tst[h] = value.astype(bf16)
    for d in (1, 2, 3):
        text_z(d).start()
    for e in (1, 2, 3):
        text_y(0, e).start()
    local_text = pltpu.make_async_copy(tst.at[zh], tkv_ref.at[blk], lsem.at[8])
    local_text.start()

    for w in wcopies[:3]:
        w.wait()

    def project(t, x_):
        p = lax.rem(x + x_, 4)
        pair = mods[pl.ds(p * 2, 2)].reshape(PAIR, mods.shape[2])
        qs = head_norm(jnp.dot(pair, wq[0], preferred_element_type=f32), gain_q)
        for h, value in enumerate(pack_heads([v[0:ROWS] for v in qs], [v[ROWS:PAIR] for v in qs])):
            qst[t, h] = value.astype(bf16)
        ks = head_norm(jnp.dot(pair, wq[1], preferred_element_type=f32), gain_k)
        vs = jnp.dot(pair, wq[2], preferred_element_type=f32)
        for h, value in enumerate(pack_heads(ks, [vs[:, 0:128], vs[:, 128:256]])):
            kvst[t, h] = value.astype(bf16)
        for d in (2, 1, 3):
            copy_kv(t, p, d).start()
        for d in (2, 1, 3):
            copy_q(t, p, d).start()
        for e in (2, 1, 3):
            copy_y(t, p, 0, e).start()
        pltpu.make_async_copy(kvst.at[t, zh], kv_ref.at[blk, p], lsem.at[t]).start()
        pltpu.make_async_copy(qst.at[t, zh], q_ref.at[zh, p], lsem.at[4 + t]).start()

    def pass_on(t, x_):
        p = lax.rem(x + x_, 4)
        for d in (1, 3, 2):
            landed_kv(t, p, d).wait_recv()
            for e in (2, 1, 3):
                copy_y(t, p, d, e).start()

    arrive[0].wait_recv()
    sends[3].start()
    sends[4].start()
    arrive[1].wait_recv()
    sends[5].start()
    arrive[2].wait_recv()
    sends[6].start()
    project(0, 0)
    for d in (1, 2, 3):
        text_z_landed(d).wait_recv()
        for e in (1, 2, 3):
            text_y(d, e).start()
    arrive[3].wait_recv()
    sends[7].start()
    arrive[4].wait_recv()
    sends[8].start()
    project(1, 3)
    project(2, 1)
    pass_on(0, 0)
    for i in (5, 6, 7, 8):
        arrive[i].wait_recv()
    for d in (1, 3, 2):
        out_x(d).start()
    project(3, 2)
    pass_on(1, 3)
    pass_on(2, 1)
    pass_on(3, 2)

    for i in range(9):
        sends[i].wait_send()
    local_text.wait()
    own_out.wait()
    for d in (1, 2, 3):
        out_x(d).wait_send()
        out_x_landed(d).wait_recv()
    for d in (1, 2, 3):
        text_z(d).wait_send()
    for d in range(4):
        for e in (1, 2, 3):
            text_y(d, e).wait_send()
            text_y_landed(d, e).wait_recv()
    for t, x_ in enumerate((0, 3, 1, 2)):
        p = lax.rem(x + x_, 4)
        pltpu.make_async_copy(kvst.at[t, zh], kv_ref.at[blk, p], lsem.at[t]).wait()
        pltpu.make_async_copy(qst.at[t, zh], q_ref.at[zh, p], lsem.at[4 + t]).wait()
        for d in (1, 2, 3):
            copy_kv(t, p, d).wait_send()
            copy_q(t, p, d).wait_send()
            landed_q(t, p, d).wait_recv()
        for d in range(4):
            for e in (1, 2, 3):
                copy_y(t, p, d, e).wait_send()
                landed_y(t, p, d, e).wait_recv()


def project_heads(hidden, text_states, modulation, w_qkv, w_text, w_out, qk_gain):
    width = hidden.shape[2]
    vmem = pl.BlockSpec(memory_space=pltpu.VMEM)
    hbm = pl.BlockSpec(memory_space=pl.ANY)
    dma = pltpu.SemaphoreType.DMA
    return pl.pallas_call(
        project_kernel,
        out_shape=[
            jax.ShapeDtypeStruct((16, 4, PAIR, 128), bf16),
            jax.ShapeDtypeStruct((16, TXT_PAD, 128), bf16),
            jax.ShapeDtypeStruct((4, 4, ROWS, 128), bf16),
            jax.ShapeDtypeStruct((4, 128, width), bf16),
        ],
        in_specs=[vmem, vmem, vmem, hbm, hbm, hbm, vmem],
        out_specs=[hbm, hbm, hbm, hbm],
        scratch_shapes=[
            pltpu.VMEM((8, ROWS, width), bf16),
            pltpu.VMEM((3, width, 256), bf16),
            pltpu.VMEM((2, width, 256), bf16),
            pltpu.VMEM((TXT_PAD, width), bf16),
            pltpu.VMEM((4, 4, PAIR, 128), bf16),
            pltpu.VMEM((4, 4, ROWS, 128), bf16),
            pltpu.VMEM((4, TXT_PAD, 128), bf16),
            dma((5,)),
            dma((10,)),
            dma((9,)), dma((9,)),
            dma((4, 3)), dma((4, 3)),
            dma((4, 3)), dma((4, 3)),
            dma((4, 4, 3)), dma((4, 4, 3)),
            dma((3,)), dma((3,)),
            dma((4, 3)), dma((4, 3)),
            dma((3,)), dma((3,)),
        ],
        compiler_params=pltpu.CompilerParams(
            collective_id=0, has_side_effects=True, vmem_limit_bytes=56 << 20
        ),
        name="project_heads",
    )(hidden, text_states, modulation, w_qkv, w_text, w_out, qk_gain)


KEYS = 2560


def attend_kernel(
    len_ref, q_ref, kv_ref, tkv_ref, wx_ref, o_ref, w_ref,
    q2, v1, lsem, csend, crecv, usend, urecv, dsend, drecv, fsend, frecv,
):
    step = pl.program_id(0)
    c, zh, y, x, zl = coords()
    other = (1 - c, zh * 4 + y, x * 2 + zl)
    above = (c, lax.rem(zh + zl, 4) * 4 + y, x * 2 + 1 - zl)
    below = (c, lax.rem(zh + 3 + zl, 4) * 4 + y, x * 2 + 1 - zl)

    def remote(src, dst, send, recv, to):
        return pltpu.make_async_remote_copy(
            src_ref=src, dst_ref=dst, send_sem=send, recv_sem=recv,
            device_id=to, device_id_type=MESH,
        )

    def own(i):
        return pltpu.make_async_copy(wx_ref.at[i], w_ref.at[i, zl, c], lsem.at[i])

    def across(i):
        return remote(wx_ref.at[i], w_ref.at[i, zl, c], csend.at[i], crecv.at[i], other)

    def across_landed(i):
        slot = w_ref.at[i, zl, 1 - c]
        return remote(slot, slot, csend.at[i], crecv.at[i], other)

    def upwards(i):
        rows = pl.ds(0, 64)
        return remote(wx_ref.at[i, rows], w_ref.at[i, zl, c, rows], usend.at[i], urecv.at[i], above)

    def downwards(i):
        rows = pl.ds(64, 64)
        return remote(wx_ref.at[i, rows], w_ref.at[i, zl, c, rows], dsend.at[i], drecv.at[i], below)

    def from_below(i):
        slot = w_ref.at[i, 1 - zl, c, pl.ds(0, 64)]
        return remote(slot, slot, usend.at[i], urecv.at[i], above)

    def from_above(i):
        slot = w_ref.at[i, 1 - zl, c, pl.ds(64, 64)]
        return remote(slot, slot, dsend.at[i], drecv.at[i], below)

    def across_later(i):
        slot = w_ref.at[i, 1 - zl, c]
        return remote(slot, slot, fsend.at[i], frecv.at[i], other)

    def across_later_landed(i):
        slot = w_ref.at[i, 1 - zl, 1 - c]
        return remote(slot, slot, fsend.at[i], frecv.at[i], other)

    @pl.when(step == 0)
    def _():
        barrier = pltpu.get_barrier_semaphore()
        for peer in (other, above, below):
            pl.semaphore_signal(barrier, inc=1, device_id=peer, device_id_type=MESH)
        pl.semaphore_wait(barrier, 3)
        for i in range(4):
            upwards(i).start()
            downwards(i).start()
            across(i).start()
            own(i).start()

    for late in (2, 3):

        @pl.when(step == late)
        def _():
            for i in (2 * late - 4, 2 * late - 3):
                from_below(i).wait_recv()
                from_above(i).wait_recv()
                across_later(i).start()

    image = kv_ref.shape[0]
    text = tkv_ref.shape[0]

    @pl.when(step == 0)
    def _():
        def values_and_ones(block):
            wide = block.astype(f32)
            lane = lax.broadcasted_iota(jnp.int32, wide.shape, 1)
            return jnp.where(lane < HEAD, pltpu.roll(wide, HEAD, 1), 1.0).astype(bf16)

        @pl.loop(0, image // 512)
        def _(n):
            rows = pl.ds(pl.multiple_of(n * 512, 512), 512)
            v1[rows, :] = values_and_ones(kv_ref[rows, :])

        v1[image : image + text, :] = values_and_ones(tkv_ref[...])

    low = lax.broadcasted_iota(jnp.int32, (ROWS, 128), 1) < HEAD
    for p in range(4):
        packed = q_ref[0, p].astype(f32)
        q2[PAIR * p : PAIR * p + ROWS, :] = jnp.where(low, packed, 0.0).astype(bf16)
        q2[PAIR * p + ROWS : PAIR * p + PAIR, :] = jnp.where(
            low, pltpu.roll(packed, HEAD, 1), 0.0
        ).astype(bf16)
    q = q2[...]

    def fold(carry, keys, values, usable):
        top, acc = carry
        scores = lax.dot_general(q, keys, (((1,), (1,)), ((), ())), preferred_element_type=f32)
        if usable is not None:
            scores = jnp.where(usable, scores, -1e30)
        new_top = jnp.maximum(top, jnp.max(scores, axis=1, keepdims=True))
        weights = jnp.exp2(scores - new_top).astype(bf16)
        shrink = jnp.exp2(top - new_top)
        return new_top, acc * shrink + jnp.dot(weights, values, preferred_element_type=f32)

    count = q.shape[0]
    carry = (jnp.full((count, 1), -1e30, f32), jnp.zeros((count, 128), f32))

    def image_step(j, carry):
        rows = pl.ds(pl.multiple_of(j * KEYS, KEYS), KEYS)
        return fold(carry, kv_ref[rows, :], v1[rows, :], None)

    carry = lax.fori_loop(0, image // KEYS, image_step, carry)
    row = lax.broadcasted_iota(jnp.int32, (1, text), 1)
    block = row // TXT_PAD
    within = row - block * TXT_PAD
    usable = jnp.logical_and(within < TXT_ROWS, block * TXT_ROWS + within < len_ref[0])
    top, acc = fold(carry, tkv_ref[...], v1[image : image + text, :], usable)
    out = acc / acc[:, HEAD : HEAD + 1]
    high = pltpu.roll(out, HEAD, 1)
    low = lax.broadcasted_iota(jnp.int32, (FIRST, 128), 1) < HEAD
    for s in range(8):
        o_ref[0, s] = jnp.where(
            low,
            out[ROWS * s : ROWS * s + FIRST],
            high[ROWS * (s + 1) - FIRST : ROWS * (s + 1)],
        ).astype(bf16)

    @pl.when(step == 3)
    def _():
        for i in range(4):
            own(i).wait()
            across(i).wait_send()
            across_landed(i).wait_recv()
            upwards(i).wait_send()
            downwards(i).wait_send()
            across_later(i).wait_send()
            across_later_landed(i).wait_recv()


def attend(text_len, q, kv, tkv, wx):
    dma = pltpu.SemaphoreType.DMA
    image, text = kv.shape[0], tkv.shape[0]
    return pl.pallas_call(
        attend_kernel,
        grid=(4,),
        in_specs=[
            pl.BlockSpec(memory_space=pltpu.SMEM),
            pl.BlockSpec((1, 4, ROWS, 128), lambda i: (i, 0, 0, 0)),
            pl.BlockSpec((image, 128), lambda i: (0, 0)),
            pl.BlockSpec((text, 128), lambda i: (0, 0)),
            pl.BlockSpec(memory_space=pl.ANY),
        ],
        out_specs=[
            pl.BlockSpec((1, 8, FIRST, 128), lambda i: (i, 0, 0, 0)),
            pl.BlockSpec(memory_space=pl.ANY),
        ],
        out_shape=[
            jax.ShapeDtypeStruct((4, 8, FIRST, 128), bf16),
            jax.ShapeDtypeStruct((4, 2, 2) + wx.shape[1:], bf16),
        ],
        scratch_shapes=[
            pltpu.VMEM((4 * PAIR, 128), bf16),
            pltpu.VMEM((image + text, 128), bf16),
        ]
        + [dma((4,))] * 9,
        compiler_params=pltpu.CompilerParams(
            collective_id=2, has_side_effects=True, vmem_limit_bytes=44 << 20
        ),
        cost_estimate=pl.CostEstimate(
            flops=4 * 4 * 4 * PAIR * (image + text) * 128,
            bytes_accessed=3 * image * 128 * 2,
            transcendentals=4 * 4 * PAIR * (image + text),
        ),
        name="attend",
    )(text_len, q, kv, tkv, wx)


def finish_kernel(
    o_ref, hid_ref, mod_ref, wout_ref, wfinal_ref, wpatch_ref, pos_ref, lat_ref, time_ref, sigma_ref,
    guided_ref, latent_ref, next_ref,
    got, att, wo, vel, wsem, lsem, osend, orecv, vsend, vrecv,
):
    c, zh, y, x, zl = coords()
    u = x * 2 + zl
    load = pltpu.make_async_copy(wout_ref, wo, wsem.at[0])
    load.start()

    barrier = pltpu.get_barrier_semaphore()
    peers = []
    for k in range(1, 32):
        dz, du = k // 8, k % 8
        peers.append((c, lax.rem(zh + dz, 4) * 4 + y, lax.rem(u + du, 8)))
    other = (1 - c, zh * 4 + y, u)
    for peer in peers + [other]:
        pl.semaphore_signal(barrier, inc=1, device_id=peer, device_id_type=MESH)
    pl.semaphore_wait(barrier, len(peers) + 1)

    def remote(src, dst, send, recv, to):
        return pltpu.make_async_remote_copy(
            src_ref=src, dst_ref=dst, send_sem=send, recv_sem=recv,
            device_id=to, device_id_type=MESH,
        )

    def out_copy(k):
        dz, du = k // 8, k % 8
        z2, u2 = lax.rem(zh + dz, 4), lax.rem(u + du, 8)
        return remote(
            o_ref.at[z2, u2], got.at[u, zh], osend.at[k], orecv.at[k], peers[k - 1]
        )

    def in_copy(k):
        dz, du = k // 8, k % 8
        z2, u2 = lax.rem(zh + 4 - dz, 4), lax.rem(u + 8 - du, 8)
        slot = got.at[u2, z2]
        return remote(slot, slot, osend.at[k], orecv.at[k], peers[k - 1])

    for k in range(31, 0, -1):
        out_copy(k).start()
    own = pltpu.make_async_copy(o_ref.at[zh, u], got.at[u, zh], lsem.at[0])
    own.start()

    states = hid_ref[0].astype(f32)
    is_cond = c == 0
    half = pos_ref.shape[1]
    patch = wpatch_ref[...].astype(f32)
    patch = jnp.where(is_cond, patch[:, 0:half], patch[:, half : 2 * half]).astype(bf16)
    t = time_ref[0]
    sigma_now = sigma_ref[t].astype(f32) / 1000.0
    sigma_next = sigma_ref[t + 1].astype(f32) / 1000.0

    own.wait()
    for k in range(1, 32):
        in_copy(k).wait_recv()
    low = lax.broadcasted_iota(jnp.int32, (FIRST, 128), 1) < HEAD
    for s in range(8):
        for pair in range(2):
            even = got[s, 2 * pair].astype(f32)
            odd = got[s, 2 * pair + 1].astype(f32)
            columns = pl.ds(s * 256 + pair * 128, 128)
            att[0:FIRST, columns] = jnp.where(low, even, pltpu.roll(odd, HEAD, 1)).astype(bf16)
            rest = jnp.where(low, pltpu.roll(even, HEAD, 1), odd).astype(bf16)
            att[FIRST:ROWS, columns] = rest[2 * FIRST - ROWS : FIRST]
    load.wait()
    projected = jnp.dot(att[...], wo[...], preferred_element_type=f32)
    mixed = states + mod_ref[2] * projected
    final = (layer_norm(mixed) * (1.0 + mod_ref[4]) + mod_ref[3]).astype(bf16)
    velocity = lax.dot_general(
        wfinal_ref[...], final, (((1,), (1,)), ((), ())), preferred_element_type=f32
    )
    vel[0] = velocity
    exchange = remote(vel.at[0], vel.at[1], vsend.at[0], vrecv.at[0], other)
    exchange.start()
    exchange.wait()
    partner = vel[1]
    cond = jnp.where(is_cond, velocity, partner)
    uncond = jnp.where(is_cond, partner, velocity)
    guided = uncond + guidance * (cond - uncond)
    latent = lat_ref[...] + (sigma_next - sigma_now) * guided
    embedded = jnp.dot(latent.T.astype(bf16), patch, preferred_element_type=f32)
    next_ref[...] = (embedded + pos_ref[...].astype(f32)).astype(bf16)
    channels = guided_ref.shape[0]
    guided_ref[...] = jnp.where(is_cond, guided[0:channels], guided[channels:])
    latent_ref[...] = jnp.where(is_cond, latent[0:channels], latent[channels:])
    for k in range(1, 32):
        out_copy(k).wait_send()


def finish(o, hidden, modulation, whole_out, w_final, w_patch, position, latent, timestep, sigma_table):
    vmem = pl.BlockSpec(memory_space=pltpu.VMEM)
    hbm = pl.BlockSpec(memory_space=pl.ANY)
    smem = pl.BlockSpec(memory_space=pltpu.SMEM)
    dma = pltpu.SemaphoreType.DMA
    channels = latent.shape[0] // 2
    return pl.pallas_call(
        finish_kernel,
        out_shape=[
            jax.ShapeDtypeStruct((channels, ROWS), f32),
            jax.ShapeDtypeStruct((channels, ROWS), f32),
            jax.ShapeDtypeStruct(position.shape, bf16),
        ],
        in_specs=[vmem, vmem, vmem, hbm, vmem, vmem, vmem, vmem, smem, smem],
        out_specs=[vmem, vmem, vmem],
        scratch_shapes=[
            pltpu.VMEM((8, 4, FIRST, 128), bf16),
            pltpu.VMEM((ROWS, whole_out.shape[0]), bf16),
            pltpu.VMEM(whole_out.shape, bf16),
            pltpu.VMEM((2, 2 * channels, ROWS), f32),
            dma((1,)), dma((1,)),
            dma((32,)), dma((32,)),
            dma((1,)), dma((1,)),
        ],
        compiler_params=pltpu.CompilerParams(
            collective_id=1, has_side_effects=True, vmem_limit_bytes=40 << 20
        ),
        name="finish",
    )(o, hidden, modulation, whole_out, w_final, w_patch, position, latent, timestep, sigma_table)


def body(
    hidden, text_states, modulation, w_qkv, w_text, w_out, qk_gain, w_final, w_patch,
    position, latent, text_len, timestep, sigma_table,
):
    modulation = jnp.swapaxes(modulation, 0, 1)
    kv, tkv, q, wx = project_heads(hidden, text_states, modulation, w_qkv, w_text, w_out, qk_gain)
    o, whole_out = attend(text_len, q, kv.reshape(-1, 128), tkv.reshape(-1, 128), wx)
    guided, next_latent, next_hidden = finish(
        o, hidden, modulation, whole_out.reshape(-1, w_out.shape[1]), w_final.T, w_patch,
        position, latent.T, timestep, sigma_table,
    )
    return guided.T, next_latent.T, next_hidden


def solution(mesh):
    in_specs = (
        P("cfg", ("blk", "uly"), None),
        P("cfg", "blk", None),
        P("cfg", None, None),
        P(None, None, "uly"),
        P(None, None, "uly"),
        P("uly", None),
        P(),
        P(),
        P(),
        P(("blk", "uly"), "cfg"),
        P(("blk", "uly"), None),
        P("cfg"),
        P(),
        P(),
    )
    out_specs = (P(("blk", "uly"), "cfg"), P(("blk", "uly"), "cfg"), P(("blk", "uly"), "cfg"))
    return jax.shard_map(body, mesh=mesh, in_specs=in_specs, out_specs=out_specs, check_vma=False)
```

```python
import jax
import jax.numpy as jnp
import numpy as np
from jax import lax
from jax.experimental import pallas as pl
from jax.experimental.pallas import tpu as pltpu
from jax.sharding import PartitionSpec as P

HEAD = 64
guidance = 3.5
epsilon = 1e-06
MESH = pl.DeviceIdType.MESH
bf16 = jnp.bfloat16
f32 = jnp.float32

ROWS = 80
PAIR = 160
TXT_ROWS = 21
TXT_PAD = 32
TXT_KEYS = 16 * TXT_PAD
KEYS = 16 * PAIR
QUERIES = 4 * PAIR
FIRST = 48
OUT_HALF = 128
STAGES = (0, 3, 1, 2)


def layer_norm(values):
    average = jnp.mean(values, axis=-1, keepdims=True)
    centered = values - average
    spread = jnp.mean(centered * centered, axis=-1, keepdims=True)
    return centered * lax.rsqrt(spread + epsilon)


def low_lanes(rows):
    return lax.broadcasted_iota(jnp.int32, (rows, 128), 1) < HEAD


def head_norm(values, gain):
    low = low_lanes(values.shape[0])
    columns = []
    for t in range(2):
        x = values[:, 128 * t : 128 * t + 128]
        sq = x * x
        a = jnp.sum(jnp.where(low, sq, 0.0), axis=1, keepdims=True)
        b = jnp.sum(jnp.where(low, 0.0, sq), axis=1, keepdims=True)
        scale = lax.rsqrt(jnp.where(low, a, b) * (1.0 / HEAD) + epsilon)
        columns.append(x * scale * gain)
    return columns


def pack_heads(left, right):
    low = low_lanes(left[0].shape[0])
    out = []
    for t in range(2):
        out.append(jnp.where(low, left[t], pltpu.roll(right[t], HEAD, 1)))
        out.append(jnp.where(low, pltpu.roll(left[t], HEAD, 1), right[t]))
    return out


def values_and_ones(block):
    wide = block.astype(f32)
    return jnp.where(low_lanes(wide.shape[0]), pltpu.roll(wide, HEAD, 1), 1.0).astype(bf16)


def kernel(
    hid_ref, txt_ref, mod_ref, wqkv_ref, wtext_ref, wout_ref, gain_ref, wfinal_ref, wpatch_ref,
    pos_ref, lat_ref, len_ref, time_ref, sigma_ref,
    guided_ref, latent_ref, next_ref,
    mods, wq, wt, txt, kvst, qst, tst, kvb, v1, qb, q2, tkv, tv1, top, acc, ob, got, att, wo, vel,
    wsem, lsem, bsend, brecv, zsend, zrecv, qsend, qrecv, ysend, yrecv,
    tzsend, tzrecv, tysend, tyrecv, xsend, xrecv, usend, urecv, dsend, drecv,
    csend, crecv, fsend, frecv, osend, orecv, vsend, vrecv,
):
    c = lax.axis_index("cfg")
    b = lax.axis_index("blk")
    u = lax.axis_index("uly")
    zh, y, x, zl = b // 4, b % 4, u // 2, u % 2

    def at(dz=0, dy=0, dx=0, dl=0):
        return (
            c,
            lax.rem(zh + dz, 4) * 4 + lax.rem(y + dy, 4),
            lax.rem(x + dx, 4) * 2 + lax.rem(zl + dl, 2),
        )

    other = (1 - c, b, u)
    partner, up, down = at(dl=1), at(dx=1), at(dx=3)
    above = (c, lax.rem(zh + zl, 4) * 4 + y, x * 2 + 1 - zl)
    below = (c, lax.rem(zh + 3 + zl, 4) * 4 + y, x * 2 + 1 - zl)

    qkv_in = [pltpu.make_async_copy(wqkv_ref.at[i], wq.at[i], wsem.at[i]) for i in range(3)]
    text_in = [pltpu.make_async_copy(wtext_ref.at[i], wt.at[i], wsem.at[3 + i]) for i in range(2)]
    out_in = [
        pltpu.make_async_copy(
            wout_ref.at[pl.ds(OUT_HALF * i, OUT_HALF)], wo.at[x, zl, i], wsem.at[5 + i]
        )
        for i in range(2)
    ]
    for copy in text_in + qkv_in + out_in:
        copy.start()

    barrier = pltpu.get_barrier_semaphore()
    peers = [at(dz=k // 8, dx=k % 8 // 2, dl=k % 2) for k in range(1, 32)]
    peers += [at(dy=d) for d in (1, 2, 3)] + [other]
    for peer in peers:
        pl.semaphore_signal(barrier, inc=1, device_id=peer, device_id_type=MESH)

    modulated = layer_norm(hid_ref[0].astype(f32)) * (1.0 + mod_ref[1]) + mod_ref[0]
    mods[u] = modulated.astype(bf16)
    txt[...] = jnp.zeros_like(txt)
    txt[0:TXT_ROWS, :] = txt_ref[0]
    pl.semaphore_wait(barrier, len(peers))

    def remote(src, dst, send, recv, to):
        return pltpu.make_async_remote_copy(
            src_ref=src, dst_ref=dst, send_sem=send, recv_sem=recv,
            device_id=to, device_id_type=MESH,
        )


    def shard(i, dx, dl, part, to):
        s = lax.rem(x + dx, 4) * 2 + (zl if dl == 0 else 1 - zl)
        ref = mods.at[s]
        if part == 1:
            ref = mods.at[s, pl.ds(0, FIRST)]
        elif part == 2:
            ref = mods.at[s, pl.ds(FIRST, ROWS - FIRST)]
        return remote(ref, ref, bsend.at[i], brecv.at[i], to)

    sends = [
        shard(0, 0, 0, 0, partner),
        shard(1, 0, 0, 0, up),
        shard(2, 0, 0, 0, down),
        shard(3, 0, 1, 0, up),
        shard(4, 0, 1, 0, down),
        shard(5, 3, 0, 1, up),
        shard(6, 1, 0, 2, down),
        shard(7, 3, 1, 1, up),
        shard(8, 1, 1, 2, down),
    ]
    arrive = [
        shard(0, 0, 1, 0, partner),
        shard(1, 3, 0, 0, up),
        shard(2, 1, 0, 0, down),
        shard(3, 3, 1, 0, up),
        shard(4, 1, 1, 0, down),
        shard(5, 2, 0, 1, up),
        shard(6, 2, 0, 2, down),
        shard(7, 2, 1, 1, up),
        shard(8, 2, 1, 2, down),
    ]
    for i in (0, 1, 2):
        sends[i].start()

    gain_q = gain_ref[0:1, :] * float(np.log2(np.e) * HEAD ** -0.5)
    gain_k = gain_ref[1:2, :]
    gain_q = jnp.concatenate([gain_q, gain_q], axis=1)
    gain_k = jnp.concatenate([gain_k, gain_k], axis=1)


    def source(d):
        return lax.rem(zh + 4 - d, 4) * 4 + y

    def kv_slot(t, block):
        return kvb.at[t, pl.ds(pl.multiple_of(block * PAIR, PAIR), PAIR)]

    def copy_kv(t, d):
        h = lax.rem(zh + d, 4)
        return remote(kvst.at[t, h], kv_slot(t, b), zsend.at[t, d - 1], zrecv.at[t, d - 1], at(dz=d))

    def landed_kv(t, d):
        slot = kv_slot(t, source(d))
        return remote(slot, slot, zsend.at[t, d - 1], zrecv.at[t, d - 1], at(dz=d))

    def copy_q(t, d):
        h = lax.rem(zh + d, 4)
        return remote(qst.at[t, h], qb.at[t, zh], qsend.at[t, d - 1], qrecv.at[t, d - 1], at(dz=d))

    def landed_q(t, d):
        slot = qb.at[t, lax.rem(zh + 4 - d, 4)]
        return remote(slot, slot, qsend.at[t, d - 1], qrecv.at[t, d - 1], at(dz=d))

    def copy_y(t, d, e):
        src = kvst.at[t, zh] if d == 0 else kv_slot(t, source(d))
        dst = kv_slot(t, source(d))
        return remote(src, dst, ysend.at[t, d, e - 1], yrecv.at[t, d, e - 1], at(dy=e))

    def landed_y(t, d, e):
        slot = kv_slot(t, lax.rem(zh + 4 - d, 4) * 4 + lax.rem(y + 4 - e, 4))
        return remote(slot, slot, ysend.at[t, d, e - 1], yrecv.at[t, d, e - 1], at(dy=e))

    def own_kv(t):
        return pltpu.make_async_copy(kvst.at[t, zh], kv_slot(t, b), lsem.at[t])

    def own_q(t):
        return pltpu.make_async_copy(qst.at[t, zh], qb.at[t, zh], lsem.at[4 + t])

    def text_slot(block):
        return tkv.at[pl.ds(pl.multiple_of(block * TXT_PAD, TXT_PAD), TXT_PAD)]

    def text_z(d):
        h = lax.rem(zh + d, 4)
        return remote(tst.at[h], text_slot(b), tzsend.at[d - 1], tzrecv.at[d - 1], at(dz=d))

    def text_z_landed(d):
        slot = text_slot(source(d))
        return remote(slot, slot, tzsend.at[d - 1], tzrecv.at[d - 1], at(dz=d))

    def text_y(d, e):
        src = tst.at[zh] if d == 0 else text_slot(source(d))
        return remote(src, text_slot(source(d)), tysend.at[d, e - 1], tyrecv.at[d, e - 1], at(dy=e))

    def text_y_landed(d, e):
        slot = text_slot(lax.rem(zh + 4 - d, 4) * 4 + lax.rem(y + 4 - e, 4))
        return remote(slot, slot, tysend.at[d, e - 1], tyrecv.at[d, e - 1], at(dy=e))

    own_text = pltpu.make_async_copy(tst.at[zh], text_slot(b), lsem.at[8])


    def out_x(d):
        src = wout_ref.at[pl.ds(pl.multiple_of(c * OUT_HALF, OUT_HALF), OUT_HALF)]
        return remote(src, wo.at[x, zl, c], xsend.at[d - 1], xrecv.at[d - 1], at(dx=d))

    def out_x_landed(d):
        slot = wo.at[lax.rem(x + 4 - d, 4), zl, c]
        return remote(slot, slot, xsend.at[d - 1], xrecv.at[d - 1], at(dx=d))

    half = OUT_HALF // 2

    def out_z(i):
        j = lax.rem(x + i, 4)
        copies = []
        for k, to, send, recv in ((0, above, usend, urecv), (1, below, dsend, drecv)):
            ref = wo.at[j, zl, c, pl.ds(half * k, half)]
            src = ref
            if i == 0:
                src = wout_ref.at[pl.ds(pl.multiple_of(c * OUT_HALF + half * k, half), half)]
            copies.append(remote(src, ref, send.at[i], recv.at[i], to))
        return copies

    def out_z_landed(i):
        j = lax.rem(x + i, 4)
        copies = []
        for k, to, send, recv in ((0, above, usend, urecv), (1, below, dsend, drecv)):
            ref = wo.at[j, 1 - zl, c, pl.ds(half * k, half)]
            copies.append(remote(ref, ref, send.at[i], recv.at[i], to))
        return copies

    def out_core(i, later, landed=False):
        j = lax.rem(x + i, 4)
        slot = wo.at[j, 1 - zl if later else zl, 1 - c if landed else c]
        send, recv = (fsend, frecv) if later else (csend, crecv)
        return remote(slot, slot, send.at[i], recv.at[i], other)

    def start_out_z(i):
        for copy in out_z(i):
            copy.start()

    def pass_out(i):
        for copy in out_z_landed(i):
            copy.wait_recv()
        out_core(i, True).start()


    def back(t, dx, dz, dl):
        src = ob.at[t, lax.rem(zh + dz, 4) * 2 + lax.rem(zl + dl, 2)]
        return remote(src, got.at[u, zh], osend.at[t, dz, dl], orecv.at[t, dz, dl], at(dz=dz, dx=dx, dl=dl))

    def back_landed(t, dx, dz, dl):
        slot = got.at[lax.rem(x + 4 - dx, 4) * 2 + lax.rem(zl + dl, 2), lax.rem(zh + 4 - dz, 4)]
        return remote(slot, slot, osend.at[t, dz, dl], orecv.at[t, dz, dl], at(dz=dz, dx=dx, dl=dl))

    own_back = pltpu.make_async_copy(ob.at[0, zh * 2 + zl], got.at[u, zh], lsem.at[9])

    for copy in text_in:
        copy.wait()
    rows = txt[...]
    tk = head_norm(jnp.dot(rows, wt[0], preferred_element_type=f32), gain_k)
    tv = jnp.dot(rows, wt[1], preferred_element_type=f32)
    for h, value in enumerate(pack_heads(tk, [tv[:, 0:128], tv[:, 128:256]])):
        tst[h] = value.astype(bf16)
    for d in (1, 2, 3):
        text_z(d).start()
    for e in (1, 2, 3):
        text_y(0, e).start()
    own_text.start()
    for copy in qkv_in:
        copy.wait()

    def project(t):
        p = lax.rem(x + STAGES[t], 4)
        pair = mods[pl.ds(p * 2, 2)].reshape(PAIR, mods.shape[2])
        ks = head_norm(jnp.dot(pair, wq[1], preferred_element_type=f32), gain_k)
        vs = jnp.dot(pair, wq[2], preferred_element_type=f32)
        for h, value in enumerate(pack_heads(ks, [vs[:, 0:128], vs[:, 128:256]])):
            kvst[t, h] = value.astype(bf16)
        for d in (2, 1, 3):
            copy_kv(t, d).start()
        for e in (2, 1, 3):
            copy_y(t, 0, e).start()
        own_kv(t).start()
        qs = head_norm(jnp.dot(pair, wq[0], preferred_element_type=f32), gain_q)
        for h, value in enumerate(pack_heads([v[0:ROWS] for v in qs], [v[ROWS:PAIR] for v in qs])):
            qst[t, h] = value.astype(bf16)
        for d in (2, 1, 3):
            copy_q(t, d).start()
        own_q(t).start()

    def pass_on(t):
        for d in (1, 3, 2):
            landed_kv(t, d).wait_recv()
            for e in (2, 1, 3):
                copy_y(t, d, e).start()

    arrive[0].wait_recv()
    sends[3].start()
    sends[4].start()
    arrive[1].wait_recv()
    sends[5].start()
    arrive[2].wait_recv()
    sends[6].start()
    project(0)
    for d in (1, 2, 3):
        text_z_landed(d).wait_recv()
        for e in (1, 2, 3):
            text_y(d, e).start()
    arrive[3].wait_recv()
    sends[7].start()
    arrive[4].wait_recv()
    sends[8].start()
    project(1)
    pass_on(0)
    project(2)
    own_text.wait()
    for d in range(4):
        for e in (1, 2, 3):
            text_y_landed(d, e).wait_recv()
    tv1[...] = values_and_ones(tkv[...])
    for i in (5, 6, 7, 8):
        arrive[i].wait_recv()
    out_x(1).start()
    out_x(3).start()
    project(3)
    pass_on(1)

    def fold(carry, q, keys, values, usable):
        high, total = carry
        scores = lax.dot_general(q, keys, (((1,), (1,)), ((), ())), preferred_element_type=f32)
        if usable is not None:
            scores = jnp.where(usable, scores, -1e30)
        new_high = jnp.maximum(high, jnp.max(scores, axis=1, keepdims=True))
        weights = jnp.exp2(scores - new_high).astype(bf16)
        shrink = jnp.exp2(high - new_high)
        return new_high, total * shrink + jnp.dot(weights, values, preferred_element_type=f32)

    row = lax.broadcasted_iota(jnp.int32, (1, TXT_KEYS), 1)
    block = row // TXT_PAD
    within = row - block * TXT_PAD
    usable = jnp.logical_and(within < TXT_ROWS, block * TXT_ROWS + within < len_ref[0])

    def stage(s, _):
        @pl.when(s == 1)
        def _():
            pass_on(2)
            start_out_z(0)
            out_x(2).start()

        @pl.when(s == 2)
        def _():
            for i in (1, 3):
                out_x_landed(i).wait_recv()
            for i in (1, 3):
                start_out_z(i)
                out_core(i, False).start()

        @pl.when(s == 3)
        def _():
            out_x_landed(2).wait_recv()
            start_out_z(2)
            out_core(2, False).start()

        own_q(s).wait()
        for d in (1, 2, 3):
            landed_q(s, d).wait_recv()
        low = low_lanes(ROWS)
        for p in range(4):
            packed = qb[s, p].astype(f32)
            q2[s, PAIR * p : PAIR * p + ROWS, :] = jnp.where(low, packed, 0.0).astype(bf16)
            q2[s, PAIR * p + ROWS : PAIR * p + PAIR, :] = jnp.where(
                low, pltpu.roll(packed, HEAD, 1), 0.0
            ).astype(bf16)
        first = (jnp.full((QUERIES, 1), -1e30, f32), jnp.zeros((QUERIES, 128), f32))
        top[s], acc[s] = fold(first, q2[s], tkv[...], tv1[...], usable)
        own_kv(s).wait()
        for d in range(4):
            for e in (1, 2, 3):
                landed_y(s, d, e).wait_recv()

        @pl.loop(0, KEYS // 512)
        def _(n):
            rows = pl.ds(pl.multiple_of(n * 512, 512), 512)
            v1[s, rows] = values_and_ones(kvb[s, rows])

        def unit(j, _):
            i = jnp.minimum(j, s)
            k = jnp.where(j < s, s, j - s)
            high, total = fold((top[i], acc[i]), q2[i], kvb[k], v1[k], None)
            top[i] = high
            acc[i] = total

            @pl.when(jnp.logical_and(s == 1, j == 0))
            def _():
                pass_on(3)

            @pl.when(jnp.logical_and(s == 2, j == 3))
            def _():
                pass_out(0)

            @pl.when(jnp.logical_and(s == 3, j == 3))
            def _():
                pass_out(1)
                pass_out(3)

            @pl.when(jnp.logical_and(s == 3, jnp.logical_or(j < 3, j == 6)))
            def _():
                out = acc[i]
                out = out / out[:, HEAD : HEAD + 1]
                turned = pltpu.roll(out, HEAD, 1)
                low = low_lanes(FIRST)
                for n in range(8):
                    ob[i, n] = jnp.where(
                        low,
                        out[ROWS * n : ROWS * n + FIRST],
                        turned[ROWS * (n + 1) - FIRST : ROWS * (n + 1)],
                    ).astype(bf16)
                for t in range(4):

                    @pl.when(i == t)
                    def _():
                        for dz in (2, 1, 3, 0):
                            for dl in range(2):
                                if t + dz + dl == 0:
                                    own_back.start()
                                else:
                                    back(t, STAGES[t], dz, dl).start()

            return 0

        lax.fori_loop(0, 2 * s + 1, unit, 0)
        return 0

    lax.fori_loop(0, 4, stage, 0)

    is_cond = c == 0
    width = pos_ref.shape[1]
    patch = wpatch_ref[...].astype(f32)
    patch = jnp.where(is_cond, patch[:, 0:width], patch[:, width : 2 * width]).astype(bf16)
    t_now = time_ref[0]
    sigma_now = sigma_ref[t_now].astype(f32) / 1000.0
    sigma_next = sigma_ref[t_now + 1].astype(f32) / 1000.0

    def collect(t):
        j = lax.rem(x + 4 - STAGES[t], 4)
        for dz in range(4):
            for dl in range(2):
                if t + dz + dl == 0:
                    own_back.wait()
                else:
                    back_landed(t, STAGES[t], dz, dl).wait_recv()
        low = low_lanes(FIRST)
        for l in range(2):
            for pair in range(2):
                even = got[j * 2 + l, 2 * pair].astype(f32)
                odd = got[j * 2 + l, 2 * pair + 1].astype(f32)
                columns = pl.ds(l * 256 + pair * 128, 128)
                att[j, 0:FIRST, columns] = jnp.where(low, even, pltpu.roll(odd, HEAD, 1)).astype(bf16)
                rest = jnp.where(low, pltpu.roll(even, HEAD, 1), odd).astype(bf16)
                att[j, FIRST:ROWS, columns] = rest[2 * FIRST - ROWS : FIRST]

    def weights_there(t):
        i = (4 - STAGES[t]) % 4
        if i == 0:
            for copy in out_in:
                copy.wait()
        else:
            out_core(i, False, True).wait_recv()
        out_core(i, True, True).wait_recv()

    def partial(t):
        j = lax.rem(x + 4 - STAGES[t], 4)
        return jnp.dot(att[j], wo[j].reshape(4 * OUT_HALF, wo.shape[4]), preferred_element_type=f32)

    pass_out(2)
    for t in range(3):
        collect(t)
        weights_there(t)
    projected = partial(0) + partial(1) + partial(2)
    collect(3)
    weights_there(3)
    projected = projected + partial(3)
    mixed = hid_ref[0].astype(f32) + mod_ref[2] * projected
    final = (layer_norm(mixed) * (1.0 + mod_ref[4]) + mod_ref[3]).astype(bf16)
    velocity = lax.dot_general(
        wfinal_ref[...], final, (((1,), (1,)), ((), ())), preferred_element_type=f32
    )
    vel[0] = velocity
    exchange = remote(vel.at[0], vel.at[1], vsend.at[0], vrecv.at[0], other)
    exchange.start()

    for i in range(9):
        sends[i].wait_send()
    for d in (1, 2, 3):
        text_z(d).wait_send()
        out_x(d).wait_send()
        out_core(d, False).wait_send()
    for d in range(4):
        for e in (1, 2, 3):
            text_y(d, e).wait_send()
        for copy in out_z(d):
            copy.wait_send()
        out_core(d, True).wait_send()
    for t in range(4):
        for d in (1, 2, 3):
            copy_kv(t, d).wait_send()
            copy_q(t, d).wait_send()
        for d in range(4):
            for e in (1, 2, 3):
                copy_y(t, d, e).wait_send()
            for dl in range(2):
                if t + d + dl > 0:
                    back(t, STAGES[t], d, dl).wait_send()

    exchange.wait()
    others = vel[1]
    cond = jnp.where(is_cond, velocity, others)
    uncond = jnp.where(is_cond, others, velocity)
    guided = uncond + guidance * (cond - uncond)
    latent = lat_ref[...] + (sigma_next - sigma_now) * guided
    embedded = jnp.dot(latent.T.astype(bf16), patch, preferred_element_type=f32)
    next_ref[...] = (embedded + pos_ref[...].astype(f32)).astype(bf16)
    channels = guided_ref.shape[0]
    guided_ref[...] = jnp.where(is_cond, guided[0:channels], guided[channels:])
    latent_ref[...] = jnp.where(is_cond, latent[0:channels], latent[channels:])


def body(
    hidden, text_states, modulation, w_qkv, w_text, w_out, qk_gain, w_final, w_patch,
    position, latent, text_len, timestep, sigma_table,
):
    width = hidden.shape[2]
    channels = latent.shape[1] // 2
    vmem = pl.BlockSpec(memory_space=pltpu.VMEM)
    hbm = pl.BlockSpec(memory_space=pl.ANY)
    smem = pl.BlockSpec(memory_space=pltpu.SMEM)
    dma = pltpu.SemaphoreType.DMA
    guided, next_latent, next_hidden = pl.pallas_call(
        kernel,
        out_shape=[
            jax.ShapeDtypeStruct((channels, ROWS), f32),
            jax.ShapeDtypeStruct((channels, ROWS), f32),
            jax.ShapeDtypeStruct(position.shape, bf16),
        ],
        in_specs=[vmem, vmem, vmem, hbm, hbm, hbm, vmem, vmem, vmem, vmem, vmem, smem, smem, smem],
        out_specs=[vmem, vmem, vmem],
        scratch_shapes=[
            pltpu.VMEM((8, ROWS, width), bf16),
            pltpu.VMEM((3, width, 256), bf16),
            pltpu.VMEM((2, width, 256), bf16),
            pltpu.VMEM((TXT_PAD, width), bf16),
            pltpu.VMEM((4, 4, PAIR, 128), bf16),
            pltpu.VMEM((4, 4, ROWS, 128), bf16),
            pltpu.VMEM((4, TXT_PAD, 128), bf16),
            pltpu.VMEM((4, KEYS, 128), bf16),
            pltpu.VMEM((4, KEYS, 128), bf16),
            pltpu.VMEM((4, 4, ROWS, 128), bf16),
            pltpu.VMEM((4, QUERIES, 128), bf16),
            pltpu.VMEM((TXT_KEYS, 128), bf16),
            pltpu.VMEM((TXT_KEYS, 128), bf16),
            pltpu.VMEM((4, QUERIES, 1), f32),
            pltpu.VMEM((4, QUERIES, 128), f32),
            pltpu.VMEM((4, 8, FIRST, 128), bf16),
            pltpu.VMEM((8, 4, FIRST, 128), bf16),
            pltpu.VMEM((4, ROWS, 4 * OUT_HALF), bf16),
            pltpu.VMEM((4, 2, 2, OUT_HALF, width), bf16),
            pltpu.VMEM((2, 2 * channels, ROWS), f32),
            dma((7,)), dma((10,)),
            dma((9,)), dma((9,)),
            dma((4, 3)), dma((4, 3)),
            dma((4, 3)), dma((4, 3)),
            dma((4, 4, 3)), dma((4, 4, 3)),
            dma((3,)), dma((3,)),
            dma((4, 3)), dma((4, 3)),
            dma((3,)), dma((3,)),
            dma((4,)), dma((4,)), dma((4,)), dma((4,)),
            dma((4,)), dma((4,)), dma((4,)), dma((4,)),
            dma((4, 4, 2)), dma((4, 4, 2)),
            dma((1,)), dma((1,)),
        ],
        compiler_params=pltpu.CompilerParams(
            collective_id=0, has_side_effects=True, vmem_limit_bytes=60 << 20
        ),
        name="sublayer",
    )(
        hidden, text_states, jnp.swapaxes(modulation, 0, 1), w_qkv, w_text, w_out, qk_gain,
        w_final.T, w_patch, position, latent.T, text_len, timestep, sigma_table,
    )
    return guided.T, next_latent.T, next_hidden


def solution(mesh):
    in_specs = (
        P("cfg", ("blk", "uly"), None),
        P("cfg", "blk", None),
        P("cfg", None, None),
        P(None, None, "uly"),
        P(None, None, "uly"),
        P("uly", None),
        P(),
        P(),
        P(),
        P(("blk", "uly"), "cfg"),
        P(("blk", "uly"), None),
        P("cfg"),
        P(),
        P(),
    )
    out_specs = (P(("blk", "uly"), "cfg"), P(("blk", "uly"), "cfg"), P(("blk", "uly"), "cfg"))
    return jax.shard_map(body, mesh=mesh, in_specs=in_specs, out_specs=out_specs, check_vma=False)
```

```python
import jax
import jax.numpy as jnp
import numpy as np
from jax import lax
from jax.experimental import pallas as pl
from jax.experimental.pallas import tpu as pltpu
from jax.sharding import PartitionSpec as P

HEAD = 64
guidance = 3.5
epsilon = 1e-06
MESH = pl.DeviceIdType.MESH
bf16 = jnp.bfloat16
f32 = jnp.float32

ROWS = 80
PAIR = 160
TXT_ROWS = 21
TXT_PAD = 32
TXT_KEYS = 16 * TXT_PAD
KEYS = 16 * PAIR
QUERIES = 4 * PAIR
FIRST = 48
OUT_HALF = 128
STAGES = (((0, 0), (0, 1)), ((3, 0), (1, 0)), ((3, 1), (1, 1)), ((2, 0), (2, 1)))


def layer_norm(values):
    average = jnp.mean(values, axis=-1, keepdims=True)
    centered = values - average
    spread = jnp.mean(centered * centered, axis=-1, keepdims=True)
    return centered * lax.rsqrt(spread + epsilon)


def low_lanes(rows):
    return lax.broadcasted_iota(jnp.int32, (rows, 128), 1) < HEAD


def head_norm(values, gain):
    low = low_lanes(values.shape[0])
    columns = []
    for t in range(2):
        x = values[:, 128 * t : 128 * t + 128]
        sq = x * x
        a = jnp.sum(jnp.where(low, sq, 0.0), axis=1, keepdims=True)
        b = jnp.sum(jnp.where(low, 0.0, sq), axis=1, keepdims=True)
        scale = lax.rsqrt(jnp.where(low, a, b) * (1.0 / HEAD) + epsilon)
        columns.append(x * scale * gain)
    return columns


def pack_heads(left, right):
    low = low_lanes(left[0].shape[0])
    out = []
    for t in range(2):
        out.append(jnp.where(low, left[t], pltpu.roll(right[t], HEAD, 1)))
        out.append(jnp.where(low, pltpu.roll(left[t], HEAD, 1), right[t]))
    return out


def values_and_ones(block):
    wide = block.astype(f32)
    return jnp.where(low_lanes(wide.shape[0]), pltpu.roll(wide, HEAD, 1), 1.0).astype(bf16)


def kernel(
    hid_ref, txt_ref, mod_ref, wqkv_ref, wtext_ref, wout_ref, gain_ref, wfinal_ref, wpatch_ref,
    pos_ref, lat_ref, len_ref, time_ref, sigma_ref,
    guided_ref, latent_ref, next_ref,
    mods, wq, wt, txt, kvst, qst, tst, kvb, v1, qb, q2, tkv, tv1, top, acc, ob, got, att, wo, vel,
    wsem, lsem, bsend, brecv, zsend, zrecv, qsend, qrecv, ysend, yrecv,
    tzsend, tzrecv, tysend, tyrecv, xsend, xrecv, usend, urecv, dsend, drecv,
    csend, crecv, fsend, frecv, osend, orecv, vsend, vrecv,
):
    c = lax.axis_index("cfg")
    b = lax.axis_index("blk")
    u = lax.axis_index("uly")
    zh, y, x, zl = b // 4, b % 4, u // 2, u % 2

    def at(dz=0, dy=0, dx=0, dl=0):
        return (
            c,
            lax.rem(zh + dz, 4) * 4 + lax.rem(y + dy, 4),
            lax.rem(x + dx, 4) * 2 + lax.rem(zl + dl, 2),
        )

    other = (1 - c, b, u)
    partner, up, down = at(dl=1), at(dx=1), at(dx=3)
    above = (c, lax.rem(zh + zl, 4) * 4 + y, x * 2 + 1 - zl)
    below = (c, lax.rem(zh + 3 + zl, 4) * 4 + y, x * 2 + 1 - zl)

    qkv_in = [pltpu.make_async_copy(wqkv_ref.at[i], wq.at[i], wsem.at[i]) for i in range(3)]
    text_in = [pltpu.make_async_copy(wtext_ref.at[i], wt.at[i], wsem.at[3 + i]) for i in range(2)]
    out_in = [
        pltpu.make_async_copy(
            wout_ref.at[pl.ds(OUT_HALF * i, OUT_HALF)], wo.at[x, zl, i], wsem.at[5 + i]
        )
        for i in range(2)
    ]
    for copy in text_in + qkv_in + out_in:
        copy.start()

    barrier = pltpu.get_barrier_semaphore()
    peers = [at(dz=k // 8, dx=k % 8 // 2, dl=k % 2) for k in range(1, 32)]
    peers += [at(dy=d) for d in (1, 2, 3)] + [other]
    for peer in peers:
        pl.semaphore_signal(barrier, inc=1, device_id=peer, device_id_type=MESH)

    modulated = layer_norm(hid_ref[0].astype(f32)) * (1.0 + mod_ref[1]) + mod_ref[0]
    mods[u] = modulated.astype(bf16)
    txt[...] = jnp.zeros_like(txt)
    txt[0:TXT_ROWS, :] = txt_ref[0]
    pl.semaphore_wait(barrier, len(peers))

    def remote(src, dst, send, recv, to):
        return pltpu.make_async_remote_copy(
            src_ref=src, dst_ref=dst, send_sem=send, recv_sem=recv,
            device_id=to, device_id_type=MESH,
        )


    def shard(i, dx, dl, part, to):
        s = lax.rem(x + dx, 4) * 2 + (zl if dl == 0 else 1 - zl)
        ref = mods.at[s]
        if part == 1:
            ref = mods.at[s, pl.ds(0, FIRST)]
        elif part == 2:
            ref = mods.at[s, pl.ds(FIRST, ROWS - FIRST)]
        return remote(ref, ref, bsend.at[i], brecv.at[i], to)

    sends = [
        shard(0, 0, 0, 0, partner),
        shard(1, 0, 0, 0, up),
        shard(2, 0, 0, 0, down),
        shard(3, 0, 1, 0, up),
        shard(4, 0, 1, 0, down),
        shard(5, 3, 0, 1, up),
        shard(6, 1, 0, 2, down),
        shard(7, 3, 1, 1, up),
        shard(8, 1, 1, 2, down),
    ]
    arrive = [
        shard(0, 0, 1, 0, partner),
        shard(1, 3, 0, 0, up),
        shard(2, 1, 0, 0, down),
        shard(3, 3, 1, 0, up),
        shard(4, 1, 1, 0, down),
        shard(5, 2, 0, 1, up),
        shard(6, 2, 0, 2, down),
        shard(7, 2, 1, 1, up),
        shard(8, 2, 1, 2, down),
    ]
    for i in (0, 1, 2):
        sends[i].start()

    gain_q = gain_ref[0:1, :] * float(np.log2(np.e) * HEAD ** -0.5)
    gain_k = gain_ref[1:2, :]
    gain_q = jnp.concatenate([gain_q, gain_q], axis=1)
    gain_k = jnp.concatenate([gain_k, gain_k], axis=1)


    def source(d):
        return lax.rem(zh + 4 - d, 4) * 4 + y

    def kv_slot(t, block):
        return kvb.at[t, pl.ds(pl.multiple_of(block * PAIR, PAIR), PAIR)]

    def copy_kv(t, d):
        h = lax.rem(zh + d, 4)
        return remote(kvst.at[t, h], kv_slot(t, b), zsend.at[t, d - 1], zrecv.at[t, d - 1], at(dz=d))

    def landed_kv(t, d):
        slot = kv_slot(t, source(d))
        return remote(slot, slot, zsend.at[t, d - 1], zrecv.at[t, d - 1], at(dz=d))

    def copy_q(t, d):
        h = lax.rem(zh + d, 4)
        return remote(qst.at[t, h], qb.at[t, zh], qsend.at[t, d - 1], qrecv.at[t, d - 1], at(dz=d))

    def landed_q(t, d):
        slot = qb.at[t, lax.rem(zh + 4 - d, 4)]
        return remote(slot, slot, qsend.at[t, d - 1], qrecv.at[t, d - 1], at(dz=d))

    def copy_y(t, d, e):
        src = kvst.at[t, zh] if d == 0 else kv_slot(t, source(d))
        dst = kv_slot(t, source(d))
        return remote(src, dst, ysend.at[t, d, e - 1], yrecv.at[t, d, e - 1], at(dy=e))

    def landed_y(t, d, e):
        slot = kv_slot(t, lax.rem(zh + 4 - d, 4) * 4 + lax.rem(y + 4 - e, 4))
        return remote(slot, slot, ysend.at[t, d, e - 1], yrecv.at[t, d, e - 1], at(dy=e))

    def own_kv(t):
        return pltpu.make_async_copy(kvst.at[t, zh], kv_slot(t, b), lsem.at[t])

    def own_q(t):
        return pltpu.make_async_copy(qst.at[t, zh], qb.at[t, zh], lsem.at[4 + t])

    def text_slot(block):
        return tkv.at[pl.ds(pl.multiple_of(block * TXT_PAD, TXT_PAD), TXT_PAD)]

    def text_z(d):
        h = lax.rem(zh + d, 4)
        return remote(tst.at[h], text_slot(b), tzsend.at[d - 1], tzrecv.at[d - 1], at(dz=d))

    def text_z_landed(d):
        slot = text_slot(source(d))
        return remote(slot, slot, tzsend.at[d - 1], tzrecv.at[d - 1], at(dz=d))

    def text_y(d, e):
        src = tst.at[zh] if d == 0 else text_slot(source(d))
        return remote(src, text_slot(source(d)), tysend.at[d, e - 1], tyrecv.at[d, e - 1], at(dy=e))

    def text_y_landed(d, e):
        slot = text_slot(lax.rem(zh + 4 - d, 4) * 4 + lax.rem(y + 4 - e, 4))
        return remote(slot, slot, tysend.at[d, e - 1], tyrecv.at[d, e - 1], at(dy=e))

    own_text = pltpu.make_async_copy(tst.at[zh], text_slot(b), lsem.at[8])


    def out_x(d):
        src = wout_ref.at[pl.ds(pl.multiple_of(c * OUT_HALF, OUT_HALF), OUT_HALF)]
        return remote(src, wo.at[x, zl, c], xsend.at[d - 1], xrecv.at[d - 1], at(dx=d))

    def out_x_landed(d):
        slot = wo.at[lax.rem(x + 4 - d, 4), zl, c]
        return remote(slot, slot, xsend.at[d - 1], xrecv.at[d - 1], at(dx=d))

    half = OUT_HALF // 2

    def out_z(i):
        j = lax.rem(x + i, 4)
        copies = []
        for k, to, send, recv in ((0, above, usend, urecv), (1, below, dsend, drecv)):
            ref = wo.at[j, zl, c, pl.ds(half * k, half)]
            src = ref
            if i == 0:
                src = wout_ref.at[pl.ds(pl.multiple_of(c * OUT_HALF + half * k, half), half)]
            copies.append(remote(src, ref, send.at[i], recv.at[i], to))
        return copies

    def out_z_landed(i):
        j = lax.rem(x + i, 4)
        copies = []
        for k, to, send, recv in ((0, above, usend, urecv), (1, below, dsend, drecv)):
            ref = wo.at[j, 1 - zl, c, pl.ds(half * k, half)]
            copies.append(remote(ref, ref, send.at[i], recv.at[i], to))
        return copies

    def out_core(i, later, landed=False):
        j = lax.rem(x + i, 4)
        slot = wo.at[j, 1 - zl if later else zl, 1 - c if landed else c]
        send, recv = (fsend, frecv) if later else (csend, crecv)
        return remote(slot, slot, send.at[i], recv.at[i], other)

    def start_out_z(i):
        for copy in out_z(i):
            copy.start()

    def pass_out(i):
        for copy in out_z_landed(i):
            copy.wait_recv()
        out_core(i, True).start()


    def back(t, k, dz):
        dx, dl = STAGES[t][k]
        src = ob.at[t, lax.rem(zh + dz, 4) * 2 + k]
        return remote(src, got.at[u, zh], osend.at[t, k, dz], orecv.at[t, k, dz], at(dz=dz, dx=dx, dl=dl))

    def sender(t, k):
        dx, dl = STAGES[t][k]
        return lax.rem(x + 4 - dx, 4), lax.rem(zl + dl, 2)

    def back_landed(t, k, dz):
        dx, dl = STAGES[t][k]
        j, l = sender(t, k)
        slot = got.at[j * 2 + l, lax.rem(zh + 4 - dz, 4)]
        return remote(slot, slot, osend.at[t, k, dz], orecv.at[t, k, dz], at(dz=dz, dx=dx, dl=dl))

    own_back = pltpu.make_async_copy(ob.at[0, zh * 2], got.at[u, zh], lsem.at[9])

    for copy in text_in:
        copy.wait()
    rows = txt[...]
    tk = head_norm(jnp.dot(rows, wt[0], preferred_element_type=f32), gain_k)
    tv = jnp.dot(rows, wt[1], preferred_element_type=f32)
    for h, value in enumerate(pack_heads(tk, [tv[:, 0:128], tv[:, 128:256]])):
        tst[h] = value.astype(bf16)
    for d in (1, 2, 3):
        text_z(d).start()
    for e in (1, 2, 3):
        text_y(0, e).start()
    own_text.start()
    for copy in qkv_in:
        copy.wait()

    def project(t):
        pair = jnp.concatenate(
            [mods[lax.rem(x + dx, 4) * 2 + lax.rem(zl + dl, 2)] for dx, dl in STAGES[t]], axis=0
        )
        ks = head_norm(jnp.dot(pair, wq[1], preferred_element_type=f32), gain_k)
        vs = jnp.dot(pair, wq[2], preferred_element_type=f32)
        for h, value in enumerate(pack_heads(ks, [vs[:, 0:128], vs[:, 128:256]])):
            kvst[t, h] = value.astype(bf16)
        for d in (2, 1, 3):
            copy_kv(t, d).start()
        for e in (2, 1, 3):
            copy_y(t, 0, e).start()
        own_kv(t).start()
        qs = head_norm(jnp.dot(pair, wq[0], preferred_element_type=f32), gain_q)
        for h, value in enumerate(pack_heads([v[0:ROWS] for v in qs], [v[ROWS:PAIR] for v in qs])):
            qst[t, h] = value.astype(bf16)
        for d in (2, 1, 3):
            copy_q(t, d).start()
        own_q(t).start()

    def pass_on(t):
        for d in (1, 3, 2):
            landed_kv(t, d).wait_recv()
            for e in (2, 1, 3):
                copy_y(t, d, e).start()

    arrive[0].wait_recv()
    sends[3].start()
    sends[4].start()
    arrive[1].wait_recv()
    sends[5].start()
    arrive[2].wait_recv()
    sends[6].start()
    project(0)
    project(1)
    for d in (1, 2, 3):
        text_z_landed(d).wait_recv()
        for e in (1, 2, 3):
            text_y(d, e).start()
    pass_on(0)
    arrive[3].wait_recv()
    sends[7].start()
    arrive[4].wait_recv()
    sends[8].start()
    project(2)
    pass_on(1)
    own_text.wait()
    for d in range(4):
        for e in (1, 2, 3):
            text_y_landed(d, e).wait_recv()
    tv1[...] = values_and_ones(tkv[...])

    def fold(carry, q, keys, values, usable):
        high, total = carry
        scores = lax.dot_general(q, keys, (((1,), (1,)), ((), ())), preferred_element_type=f32)
        if usable is not None:
            scores = jnp.where(usable, scores, -1e30)
        new_high = jnp.maximum(high, jnp.max(scores, axis=1, keepdims=True))
        wide = jnp.concatenate([new_high] * (keys.shape[0] // 128), axis=1)
        weights = jnp.exp2(scores - wide).astype(bf16)
        shrink = jnp.exp2(high - new_high)
        return new_high, total * shrink + jnp.dot(weights, values, preferred_element_type=f32)

    row = lax.broadcasted_iota(jnp.int32, (1, TXT_KEYS), 1)
    block = row // TXT_PAD
    within = row - block * TXT_PAD
    usable = jnp.logical_and(within < TXT_ROWS, block * TXT_ROWS + within < len_ref[0])

    def stage(s, _):
        @pl.when(s == 1)
        def _():
            for i in (5, 6, 7, 8):
                arrive[i].wait_recv()
            out_x(1).start()
            out_x(3).start()
            project(3)
            pass_on(2)

        own_q(s).wait()
        for d in (1, 2, 3):
            landed_q(s, d).wait_recv()
        low = low_lanes(ROWS)
        for p in range(4):
            packed = qb[s, p].astype(f32)
            q2[s, PAIR * p : PAIR * p + ROWS, :] = jnp.where(low, packed, 0.0).astype(bf16)
            q2[s, PAIR * p + ROWS : PAIR * p + PAIR, :] = jnp.where(
                low, pltpu.roll(packed, HEAD, 1), 0.0
            ).astype(bf16)
        first = (jnp.full((QUERIES, 128), -1e30, f32), jnp.zeros((QUERIES, 128), f32))
        top[s], acc[s] = fold(first, q2[s], tkv[...], tv1[...], usable)
        own_kv(s).wait()
        for d in range(4):
            for e in (1, 2, 3):
                landed_y(s, d, e).wait_recv()

        @pl.loop(0, KEYS // 512)
        def _(n):
            rows = pl.ds(pl.multiple_of(n * 512, 512), 512)
            v1[s, rows] = values_and_ones(kvb[s, rows])

        def unit(j, _):
            i = jnp.minimum(j, s)
            k = jnp.where(j < s, s, j - s)
            high, total = fold((top[i], acc[i]), q2[i], kvb[k], v1[k], None)
            top[i] = high
            acc[i] = total

            @pl.when(jnp.logical_and(s == 1, j == 1))
            def _():
                pass_on(3)
                start_out_z(0)
                out_x(2).start()

            @pl.when(jnp.logical_and(s == 2, j == 1))
            def _():
                for i in (1, 3):
                    out_x_landed(i).wait_recv()
                for i in (1, 3):
                    start_out_z(i)
                    out_core(i, False).start()

            @pl.when(jnp.logical_and(s == 2, j == 3))
            def _():
                pass_out(0)

            @pl.when(jnp.logical_and(s == 3, j == 1))
            def _():
                out_x_landed(2).wait_recv()
                start_out_z(2)
                out_core(2, False).start()

            @pl.when(jnp.logical_and(s == 3, j == 4))
            def _():
                pass_out(1)
                pass_out(3)

            @pl.when(jnp.logical_and(s == 3, jnp.logical_or(j < 3, j == 6)))
            def _():
                out = acc[i]
                out = out / out[:, HEAD : HEAD + 1]
                turned = pltpu.roll(out, HEAD, 1)
                low = low_lanes(FIRST)
                for n in range(8):
                    ob[i, n] = jnp.where(
                        low,
                        out[ROWS * n : ROWS * n + FIRST],
                        turned[ROWS * (n + 1) - FIRST : ROWS * (n + 1)],
                    ).astype(bf16)
                for t in range(4):

                    @pl.when(i == t)
                    def _():
                        for dz in (2, 1, 3, 0):
                            for k in range(2):
                                if t + k + dz == 0:
                                    own_back.start()
                                else:
                                    back(t, k, dz).start()

            return 0

        lax.fori_loop(0, 2 * s + 1, unit, 0)
        return 0

    lax.fori_loop(0, 4, stage, 0)

    is_cond = c == 0
    width = pos_ref.shape[1]
    patch = wpatch_ref[...].astype(f32)
    patch = jnp.where(is_cond, patch[:, 0:width], patch[:, width : 2 * width]).astype(bf16)
    t_now = time_ref[0]
    sigma_now = sigma_ref[t_now].astype(f32) / 1000.0
    sigma_next = sigma_ref[t_now + 1].astype(f32) / 1000.0

    def collect(t):
        low = low_lanes(FIRST)
        for k in range(2):
            for dz in range(4):
                if t + k + dz == 0:
                    own_back.wait()
                else:
                    back_landed(t, k, dz).wait_recv()
            j, l = sender(t, k)
            n = j * 2 + l
            for pair in range(2):
                even = got[n, 2 * pair].astype(f32)
                odd = got[n, 2 * pair + 1].astype(f32)
                columns = pl.ds(pair * 128, 128)
                att[n, 0:FIRST, columns] = jnp.where(low, even, pltpu.roll(odd, HEAD, 1)).astype(bf16)
                rest = jnp.where(low, pltpu.roll(even, HEAD, 1), odd).astype(bf16)
                att[n, FIRST:ROWS, columns] = rest[2 * FIRST - ROWS : FIRST]

    def weights_there(t):
        for dx, dl in STAGES[t]:
            i = (4 - dx) % 4
            if dl == 1:
                out_core(i, True, True).wait_recv()
            elif i > 0:
                out_core(i, False, True).wait_recv()
            else:
                for copy in out_in:
                    copy.wait()

    def partial(t):
        total = 0.0
        for k in range(2):
            j, l = sender(t, k)
            weights = wo[j, l].reshape(2 * OUT_HALF, wo.shape[4])
            total += jnp.dot(att[j * 2 + l], weights, preferred_element_type=f32)
        return total

    pass_out(2)
    for t in range(3):
        collect(t)
        weights_there(t)
    projected = partial(0) + partial(1) + partial(2)
    collect(3)
    weights_there(3)
    projected = projected + partial(3)
    mixed = hid_ref[0].astype(f32) + mod_ref[2] * projected
    final = (layer_norm(mixed) * (1.0 + mod_ref[4]) + mod_ref[3]).astype(bf16)
    velocity = lax.dot_general(
        wfinal_ref[...], final, (((1,), (1,)), ((), ())), preferred_element_type=f32
    )
    vel[0] = velocity
    exchange = remote(vel.at[0], vel.at[1], vsend.at[0], vrecv.at[0], other)
    exchange.start()

    for i in range(9):
        sends[i].wait_send()
    for d in (1, 2, 3):
        text_z(d).wait_send()
        out_x(d).wait_send()
        out_core(d, False).wait_send()
    for d in range(4):
        for e in (1, 2, 3):
            text_y(d, e).wait_send()
        for copy in out_z(d):
            copy.wait_send()
        out_core(d, True).wait_send()
    for t in range(4):
        for d in (1, 2, 3):
            copy_kv(t, d).wait_send()
            copy_q(t, d).wait_send()
        for d in range(4):
            for e in (1, 2, 3):
                copy_y(t, d, e).wait_send()
            for k in range(2):
                if t + k + d > 0:
                    back(t, k, d).wait_send()

    exchange.wait()
    others = vel[1]
    cond = jnp.where(is_cond, velocity, others)
    uncond = jnp.where(is_cond, others, velocity)
    guided = uncond + guidance * (cond - uncond)
    latent = lat_ref[...] + (sigma_next - sigma_now) * guided
    embedded = jnp.dot(latent.T.astype(bf16), patch, preferred_element_type=f32)
    next_ref[...] = (embedded + pos_ref[...].astype(f32)).astype(bf16)
    channels = guided_ref.shape[0]
    guided_ref[...] = jnp.where(is_cond, guided[0:channels], guided[channels:])
    latent_ref[...] = jnp.where(is_cond, latent[0:channels], latent[channels:])


def body(
    hidden, text_states, modulation, w_qkv, w_text, w_out, qk_gain, w_final, w_patch,
    position, latent, text_len, timestep, sigma_table,
):
    width = hidden.shape[2]
    channels = latent.shape[1] // 2
    vmem = pl.BlockSpec(memory_space=pltpu.VMEM)
    hbm = pl.BlockSpec(memory_space=pl.ANY)
    smem = pl.BlockSpec(memory_space=pltpu.SMEM)
    dma = pltpu.SemaphoreType.DMA
    guided, next_latent, next_hidden = pl.pallas_call(
        kernel,
        out_shape=[
            jax.ShapeDtypeStruct((channels, ROWS), f32),
            jax.ShapeDtypeStruct((channels, ROWS), f32),
            jax.ShapeDtypeStruct(position.shape, bf16),
        ],
        in_specs=[vmem, vmem, vmem, hbm, hbm, hbm, vmem, vmem, vmem, vmem, vmem, smem, smem, smem],
        out_specs=[vmem, vmem, vmem],
        scratch_shapes=[
            pltpu.VMEM((8, ROWS, width), bf16),
            pltpu.VMEM((3, width, 256), bf16),
            pltpu.VMEM((2, width, 256), bf16),
            pltpu.VMEM((TXT_PAD, width), bf16),
            pltpu.VMEM((4, 4, PAIR, 128), bf16),
            pltpu.VMEM((4, 4, ROWS, 128), bf16),
            pltpu.VMEM((4, TXT_PAD, 128), bf16),
            pltpu.VMEM((4, KEYS, 128), bf16),
            pltpu.VMEM((4, KEYS, 128), bf16),
            pltpu.VMEM((4, 4, ROWS, 128), bf16),
            pltpu.VMEM((4, QUERIES, 128), bf16),
            pltpu.VMEM((TXT_KEYS, 128), bf16),
            pltpu.VMEM((TXT_KEYS, 128), bf16),
            pltpu.VMEM((4, QUERIES, 128), f32),
            pltpu.VMEM((4, QUERIES, 128), f32),
            pltpu.VMEM((4, 8, FIRST, 128), bf16),
            pltpu.VMEM((8, 4, FIRST, 128), bf16),
            pltpu.VMEM((8, ROWS, 2 * OUT_HALF), bf16),
            pltpu.VMEM((4, 2, 2, OUT_HALF, width), bf16),
            pltpu.VMEM((2, 2 * channels, ROWS), f32),
            dma((7,)), dma((10,)),
            dma((9,)), dma((9,)),
            dma((4, 3)), dma((4, 3)),
            dma((4, 3)), dma((4, 3)),
            dma((4, 4, 3)), dma((4, 4, 3)),
            dma((3,)), dma((3,)),
            dma((4, 3)), dma((4, 3)),
            dma((3,)), dma((3,)),
            dma((4,)), dma((4,)), dma((4,)), dma((4,)),
            dma((4,)), dma((4,)), dma((4,)), dma((4,)),
            dma((4, 2, 4)), dma((4, 2, 4)),
            dma((1,)), dma((1,)),
        ],
        compiler_params=pltpu.CompilerParams(
            collective_id=0, has_side_effects=True, vmem_limit_bytes=60 << 20
        ),
        name="sublayer",
    )(
        hidden, text_states, jnp.swapaxes(modulation, 0, 1), w_qkv, w_text, w_out, qk_gain,
        w_final.T, w_patch, position, latent.T, text_len, timestep, sigma_table,
    )
    return guided.T, next_latent.T, next_hidden


def solution(mesh):
    in_specs = (
        P("cfg", ("blk", "uly"), None),
        P("cfg", "blk", None),
        P("cfg", None, None),
        P(None, None, "uly"),
        P(None, None, "uly"),
        P("uly", None),
        P(),
        P(),
        P(),
        P(("blk", "uly"), "cfg"),
        P(("blk", "uly"), None),
        P("cfg"),
        P(),
        P(),
    )
    out_specs = (P(("blk", "uly"), "cfg"), P(("blk", "uly"), "cfg"), P(("blk", "uly"), "cfg"))
    return jax.shard_map(body, mesh=mesh, in_specs=in_specs, out_specs=out_specs, check_vma=False)
```

```python
import jax
import jax.numpy as jnp
import numpy as np
from jax import lax
from jax.experimental import pallas as pl
from jax.experimental.pallas import tpu as pltpu
from jax.sharding import PartitionSpec as P

HEAD = 64
guidance = 3.5
epsilon = 1e-06
MESH = pl.DeviceIdType.MESH
bf16 = jnp.bfloat16
f32 = jnp.float32

ROWS = 80
PAIR = 160
TXT_ROWS = 21
TXT_PAD = 32
TXT_KEYS = 16 * TXT_PAD
KEYS = 16 * PAIR
QUERIES = 4 * PAIR
FIRST = 48
OUT_HALF = 128
STAGES = (((0, 0), (0, 1)), ((3, 0), (1, 0)), ((3, 1), (1, 1)), ((2, 0), (2, 1)))


def layer_norm(values):
    average = jnp.mean(values, axis=-1, keepdims=True)
    centered = values - average
    spread = jnp.mean(centered * centered, axis=-1, keepdims=True)
    return centered * lax.rsqrt(spread + epsilon)


def low_lanes(rows):
    return lax.broadcasted_iota(jnp.int32, (rows, 128), 1) < HEAD


def head_norm(values, gain):
    low = low_lanes(values.shape[0])
    columns = []
    for t in range(2):
        x = values[:, 128 * t : 128 * t + 128]
        sq = x * x
        a = jnp.sum(jnp.where(low, sq, 0.0), axis=1, keepdims=True)
        b = jnp.sum(jnp.where(low, 0.0, sq), axis=1, keepdims=True)
        scale = lax.rsqrt(jnp.where(low, a, b) * (1.0 / HEAD) + epsilon)
        columns.append(x * scale * gain)
    return columns


def pack_heads(left, right):
    low = low_lanes(left[0].shape[0])
    out = []
    for t in range(2):
        out.append(jnp.where(low, left[t], pltpu.roll(right[t], HEAD, 1)))
        out.append(jnp.where(low, pltpu.roll(left[t], HEAD, 1), right[t]))
    return out


def values_and_ones(block):
    wide = block.astype(f32)
    return jnp.where(low_lanes(wide.shape[0]), pltpu.roll(wide, HEAD, 1), 1.0).astype(bf16)


def kernel(
    hid_ref, txt_ref, mod_ref, wqkv_ref, wtext_ref, wout_ref, gain_ref, wfinal_ref, wpatch_ref,
    pos_ref, lat_ref, len_ref, time_ref, sigma_ref,
    guided_ref, latent_ref, next_ref,
    mods, wq, wt, txt, kvst, qst, tst, kvb, v1, qb, q2, tkv, tv1, top, acc, ob, got, att, wo, vel,
    wsem, lsem, bsend, brecv, zsend, zrecv, qsend, qrecv, ysend, yrecv,
    tzsend, tzrecv, tysend, tyrecv, xsend, xrecv, usend, urecv, dsend, drecv,
    csend, crecv, fsend, frecv, osend, orecv, vsend, vrecv,
):
    c = lax.axis_index("cfg")
    b = lax.axis_index("blk")
    u = lax.axis_index("uly")
    zh, y, x, zl = b // 4, b % 4, u // 2, u % 2

    def at(dz=0, dy=0, dx=0, dl=0):
        return (
            c,
            lax.rem(zh + dz, 4) * 4 + lax.rem(y + dy, 4),
            lax.rem(x + dx, 4) * 2 + lax.rem(zl + dl, 2),
        )

    other = (1 - c, b, u)
    partner, up, down = at(dl=1), at(dx=1), at(dx=3)
    above = (c, lax.rem(zh + zl, 4) * 4 + y, x * 2 + 1 - zl)
    below = (c, lax.rem(zh + 3 + zl, 4) * 4 + y, x * 2 + 1 - zl)
    far = (c, lax.rem(zh + 3 + 2 * zl, 4) * 4 + y, x * 2 + 1 - zl)

    qkv_in = [pltpu.make_async_copy(wqkv_ref.at[i], wq.at[i], wsem.at[i]) for i in range(3)]
    text_in = [pltpu.make_async_copy(wtext_ref.at[i], wt.at[i], wsem.at[3 + i]) for i in range(2)]
    out_in = [
        pltpu.make_async_copy(
            wout_ref.at[pl.ds(OUT_HALF * i, OUT_HALF)], wo.at[x, zl, i], wsem.at[5 + i]
        )
        for i in range(2)
    ]
    for copy in text_in + qkv_in + out_in:
        copy.start()

    barrier = pltpu.get_barrier_semaphore()
    peers = [at(dz=k // 8, dx=k % 8 // 2, dl=k % 2) for k in range(1, 32)]
    peers += [at(dy=d) for d in (1, 2, 3)] + [other]
    for peer in peers:
        pl.semaphore_signal(barrier, inc=1, device_id=peer, device_id_type=MESH)

    modulated = layer_norm(hid_ref[0].astype(f32)) * (1.0 + mod_ref[1]) + mod_ref[0]
    mods[u] = modulated.astype(bf16)
    txt[...] = jnp.zeros_like(txt)
    txt[0:TXT_ROWS, :] = txt_ref[0]
    pl.semaphore_wait(barrier, len(peers))

    def remote(src, dst, send, recv, to):
        return pltpu.make_async_remote_copy(
            src_ref=src, dst_ref=dst, send_sem=send, recv_sem=recv,
            device_id=to, device_id_type=MESH,
        )


    def shard(i, dx, dl, part, to):
        s = lax.rem(x + dx, 4) * 2 + (zl if dl == 0 else 1 - zl)
        ref = mods.at[s]
        if part == 1:
            ref = mods.at[s, pl.ds(0, FIRST)]
        elif part == 2:
            ref = mods.at[s, pl.ds(FIRST, ROWS - FIRST)]
        return remote(ref, ref, bsend.at[i], brecv.at[i], to)

    sends = [
        shard(0, 0, 0, 0, partner),
        shard(1, 0, 0, 0, up),
        shard(2, 0, 0, 0, down),
        shard(3, 0, 1, 0, up),
        shard(4, 0, 1, 0, down),
        shard(5, 3, 0, 1, up),
        shard(6, 1, 0, 2, down),
        shard(7, 3, 1, 1, up),
        shard(8, 1, 1, 2, down),
    ]
    arrive = [
        shard(0, 0, 1, 0, partner),
        shard(1, 3, 0, 0, up),
        shard(2, 1, 0, 0, down),
        shard(3, 3, 1, 0, up),
        shard(4, 1, 1, 0, down),
        shard(5, 2, 0, 1, up),
        shard(6, 2, 0, 2, down),
        shard(7, 2, 1, 1, up),
        shard(8, 2, 1, 2, down),
    ]
    for i in (0, 1, 2):
        sends[i].start()

    gain_q = gain_ref[0:1, :] * float(np.log2(np.e) * HEAD ** -0.5)
    gain_k = gain_ref[1:2, :]
    gain_q = jnp.concatenate([gain_q, gain_q], axis=1)
    gain_k = jnp.concatenate([gain_k, gain_k], axis=1)


    def source(d):
        return lax.rem(zh + 4 - d, 4) * 4 + y

    def kv_slot(t, block):
        return kvb.at[t, pl.ds(pl.multiple_of(block * PAIR, PAIR), PAIR)]

    def copy_kv(t, d):
        h = lax.rem(zh + d, 4)
        return remote(kvst.at[t, h], kv_slot(t, b), zsend.at[t, d - 1], zrecv.at[t, d - 1], at(dz=d))

    def landed_kv(t, d):
        slot = kv_slot(t, source(d))
        return remote(slot, slot, zsend.at[t, d - 1], zrecv.at[t, d - 1], at(dz=d))

    def copy_q(t, d):
        h = lax.rem(zh + d, 4)
        return remote(qst.at[t, h], qb.at[t, zh], qsend.at[t, d - 1], qrecv.at[t, d - 1], at(dz=d))

    def landed_q(t, d):
        slot = qb.at[t, lax.rem(zh + 4 - d, 4)]
        return remote(slot, slot, qsend.at[t, d - 1], qrecv.at[t, d - 1], at(dz=d))

    def copy_y(t, d, e):
        src = kvst.at[t, zh] if d == 0 else kv_slot(t, source(d))
        dst = kv_slot(t, source(d))
        return remote(src, dst, ysend.at[t, d, e - 1], yrecv.at[t, d, e - 1], at(dy=e))

    def landed_y(t, d, e):
        slot = kv_slot(t, lax.rem(zh + 4 - d, 4) * 4 + lax.rem(y + 4 - e, 4))
        return remote(slot, slot, ysend.at[t, d, e - 1], yrecv.at[t, d, e - 1], at(dy=e))

    def own_kv(t):
        return pltpu.make_async_copy(kvst.at[t, zh], kv_slot(t, b), lsem.at[t])

    def own_q(t):
        return pltpu.make_async_copy(qst.at[t, zh], qb.at[t, zh], lsem.at[4 + t])

    def text_slot(block):
        return tkv.at[pl.ds(pl.multiple_of(block * TXT_PAD, TXT_PAD), TXT_PAD)]

    def text_z(d):
        h = lax.rem(zh + d, 4)
        return remote(tst.at[h], text_slot(b), tzsend.at[d - 1], tzrecv.at[d - 1], at(dz=d))

    def text_z_landed(d):
        slot = text_slot(source(d))
        return remote(slot, slot, tzsend.at[d - 1], tzrecv.at[d - 1], at(dz=d))

    def text_y(d, e):
        src = tst.at[zh] if d == 0 else text_slot(source(d))
        return remote(src, text_slot(source(d)), tysend.at[d, e - 1], tyrecv.at[d, e - 1], at(dy=e))

    def text_y_landed(d, e):
        slot = text_slot(lax.rem(zh + 4 - d, 4) * 4 + lax.rem(y + 4 - e, 4))
        return remote(slot, slot, tysend.at[d, e - 1], tyrecv.at[d, e - 1], at(dy=e))

    own_text = pltpu.make_async_copy(tst.at[zh], text_slot(b), lsem.at[8])


    def out_x(d):
        src = wout_ref.at[pl.ds(pl.multiple_of(c * OUT_HALF, OUT_HALF), OUT_HALF)]
        return remote(src, wo.at[x, zl, c], xsend.at[d - 1], xrecv.at[d - 1], at(dx=d))

    def out_x_landed(d):
        slot = wo.at[lax.rem(x + 4 - d, 4), zl, c]
        return remote(slot, slot, xsend.at[d - 1], xrecv.at[d - 1], at(dx=d))

    half = OUT_HALF // 2

    def out_x_on(k):
        dx, to = ((3, up), (1, down))[k]
        ref = wo.at[lax.rem(x + dx, 4), zl, c, pl.ds(half * k, half)]
        return remote(ref, ref, xsend.at[1 + 2 * k], xrecv.at[1 + 2 * k], to)

    def out_x_on_landed(k):
        ref = wo.at[lax.rem(x + 2, 4), zl, c, pl.ds(half * k, half)]
        return remote(ref, ref, xsend.at[1 + 2 * k], xrecv.at[1 + 2 * k], (up, down)[k])

    def out_far():
        src = wout_ref.at[pl.ds(pl.multiple_of(c * OUT_HALF, OUT_HALF), OUT_HALF)]
        return remote(src, wo.at[x, zl, c], usend.at[0], urecv.at[0], far)

    def out_z(i):
        if i == 0:
            return [out_far()]
        j = lax.rem(x + i, 4)
        copies = []
        for k, to, send, recv in ((0, above, usend, urecv), (1, below, dsend, drecv)):
            ref = wo.at[j, zl, c, pl.ds(half * k, half)]
            copies.append(remote(ref, ref, send.at[i], recv.at[i], to))
        return copies

    def out_z_landed(i):
        j = lax.rem(x + i, 4)
        if i == 0:
            ref = wo.at[x, 1 - zl, c]
            return [remote(ref, ref, usend.at[0], urecv.at[0], far)]
        copies = []
        for k, to, send, recv in ((0, above, usend, urecv), (1, below, dsend, drecv)):
            ref = wo.at[j, 1 - zl, c, pl.ds(half * k, half)]
            copies.append(remote(ref, ref, send.at[i], recv.at[i], to))
        return copies

    def out_core(i, later, landed=False):
        j = lax.rem(x + i, 4)
        slot = wo.at[j, 1 - zl if later else zl, 1 - c if landed else c]
        send, recv = (fsend, frecv) if later else (csend, crecv)
        return remote(slot, slot, send.at[i], recv.at[i], other)

    def start_out_z(i):
        for copy in out_z(i):
            copy.start()

    def pass_out(i):
        for copy in out_z_landed(i):
            copy.wait_recv()
        out_core(i, True).start()


    def back(t, k, dz):
        dx, dl = STAGES[t][k]
        src = ob.at[t, lax.rem(zh + dz, 4) * 2 + k]
        return remote(src, got.at[u, zh], osend.at[t, k, dz], orecv.at[t, k, dz], at(dz=dz, dx=dx, dl=dl))

    def sender(t, k):
        dx, dl = STAGES[t][k]
        return lax.rem(x + 4 - dx, 4), lax.rem(zl + dl, 2)

    def back_landed(t, k, dz):
        dx, dl = STAGES[t][k]
        j, l = sender(t, k)
        slot = got.at[j * 2 + l, lax.rem(zh + 4 - dz, 4)]
        return remote(slot, slot, osend.at[t, k, dz], orecv.at[t, k, dz], at(dz=dz, dx=dx, dl=dl))

    own_back = pltpu.make_async_copy(ob.at[0, zh * 2], got.at[u, zh], lsem.at[9])

    for copy in text_in:
        copy.wait()
    rows = txt[...]
    tk = head_norm(jnp.dot(rows, wt[0], preferred_element_type=f32), gain_k)
    tv = jnp.dot(rows, wt[1], preferred_element_type=f32)
    for h, value in enumerate(pack_heads(tk, [tv[:, 0:128], tv[:, 128:256]])):
        tst[h] = value.astype(bf16)
    for d in (1, 2, 3):
        text_z(d).start()
    for e in (1, 2, 3):
        text_y(0, e).start()
    own_text.start()
    for copy in qkv_in:
        copy.wait()

    def project(t):
        pair = jnp.concatenate(
            [mods[lax.rem(x + dx, 4) * 2 + lax.rem(zl + dl, 2)] for dx, dl in STAGES[t]], axis=0
        )
        ks = head_norm(jnp.dot(pair, wq[1], preferred_element_type=f32), gain_k)
        vs = jnp.dot(pair, wq[2], preferred_element_type=f32)
        for h, value in enumerate(pack_heads(ks, [vs[:, 0:128], vs[:, 128:256]])):
            kvst[t, h] = value.astype(bf16)
        for d in (2, 1, 3):
            copy_kv(t, d).start()
        for e in (2, 1, 3):
            copy_y(t, 0, e).start()
        own_kv(t).start()
        qs = head_norm(jnp.dot(pair, wq[0], preferred_element_type=f32), gain_q)
        for h, value in enumerate(pack_heads([v[0:ROWS] for v in qs], [v[ROWS:PAIR] for v in qs])):
            qst[t, h] = value.astype(bf16)
        for d in (2, 1, 3):
            copy_q(t, d).start()
        own_q(t).start()

    def pass_on(t):
        for d in (1, 3, 2):
            landed_kv(t, d).wait_recv()
            for e in (2, 1, 3):
                copy_y(t, d, e).start()

    arrive[0].wait_recv()
    sends[3].start()
    sends[4].start()
    arrive[1].wait_recv()
    sends[5].start()
    arrive[2].wait_recv()
    sends[6].start()
    project(0)
    project(1)
    for d in (1, 2, 3):
        text_z_landed(d).wait_recv()
        for e in (1, 2, 3):
            text_y(d, e).start()
    pass_on(0)
    arrive[3].wait_recv()
    sends[7].start()
    arrive[4].wait_recv()
    sends[8].start()
    project(2)
    pass_on(1)
    own_text.wait()
    for d in range(4):
        for e in (1, 2, 3):
            text_y_landed(d, e).wait_recv()
    tv1[...] = values_and_ones(tkv[...])

    def fold(carry, q, keys, values, usable):
        high, total = carry
        scores = lax.dot_general(q, keys, (((1,), (1,)), ((), ())), preferred_element_type=f32)
        if usable is not None:
            scores = jnp.where(usable, scores, -1e30)
        new_high = jnp.maximum(high, jnp.max(scores, axis=1, keepdims=True))
        wide = jnp.concatenate([new_high] * (keys.shape[0] // 128), axis=1)
        weights = jnp.exp2(scores - wide).astype(bf16)
        shrink = jnp.exp2(high - new_high)
        return new_high, total * shrink + jnp.dot(weights, values, preferred_element_type=f32)

    row = lax.broadcasted_iota(jnp.int32, (1, TXT_KEYS), 1)
    block = row // TXT_PAD
    within = row - block * TXT_PAD
    usable = jnp.logical_and(within < TXT_ROWS, block * TXT_ROWS + within < len_ref[0])

    def stage(s, _):
        @pl.when(s == 1)
        def _():
            for i in (5, 6, 7, 8):
                arrive[i].wait_recv()
            out_x(1).start()
            out_x(3).start()
            project(3)
            pass_on(2)

        own_q(s).wait()
        for d in (1, 2, 3):
            landed_q(s, d).wait_recv()
        low = low_lanes(ROWS)
        for p in range(4):
            packed = qb[s, p].astype(f32)
            q2[s, PAIR * p : PAIR * p + ROWS, :] = jnp.where(low, packed, 0.0).astype(bf16)
            q2[s, PAIR * p + ROWS : PAIR * p + PAIR, :] = jnp.where(
                low, pltpu.roll(packed, HEAD, 1), 0.0
            ).astype(bf16)
        first = (jnp.full((QUERIES, 128), -1e30, f32), jnp.zeros((QUERIES, 128), f32))
        top[s], acc[s] = fold(first, q2[s], tkv[...], tv1[...], usable)
        own_kv(s).wait()
        for d in range(4):
            for e in (1, 2, 3):
                landed_y(s, d, e).wait_recv()

        @pl.loop(0, KEYS // 512)
        def _(n):
            rows = pl.ds(pl.multiple_of(n * 512, 512), 512)
            v1[s, rows] = values_and_ones(kvb[s, rows])

        def unit(j, _):
            i = jnp.minimum(j, s)
            k = jnp.where(j < s, s, j - s)
            high, total = fold((top[i], acc[i]), q2[i], kvb[k], v1[k], None)
            top[i] = high
            acc[i] = total

            @pl.when(jnp.logical_and(s == 1, j == 1))
            def _():
                pass_on(3)
                out_far().start()

            @pl.when(jnp.logical_and(s == 2, j == 2))
            def _():
                for i in (1, 3):
                    out_x_landed(i).wait_recv()
                for k in (0, 1):
                    out_x_on(k).start()
                for i in (1, 3):
                    start_out_z(i)
                    out_core(i, False).start()

            @pl.when(jnp.logical_and(s == 3, j == 0))
            def _():
                pass_out(0)
                for k in (0, 1):
                    out_x_on_landed(k).wait_recv()
                start_out_z(2)
                out_core(2, False).start()

            @pl.when(jnp.logical_and(s == 3, j == 4))
            def _():
                pass_out(1)
                pass_out(3)

            @pl.when(jnp.logical_and(s == 3, jnp.logical_or(j < 3, j == 6)))
            def _():
                out = acc[i]
                out = out / out[:, HEAD : HEAD + 1]
                turned = pltpu.roll(out, HEAD, 1)
                low = low_lanes(FIRST)
                for n in range(8):
                    ob[i, n] = jnp.where(
                        low,
                        out[ROWS * n : ROWS * n + FIRST],
                        turned[ROWS * (n + 1) - FIRST : ROWS * (n + 1)],
                    ).astype(bf16)
                for t in range(4):

                    @pl.when(i == t)
                    def _():
                        for dz in (2, 1, 3, 0):
                            for k in range(2):
                                if t + k + dz == 0:
                                    own_back.start()
                                else:
                                    back(t, k, dz).start()

            return 0

        lax.fori_loop(0, 2 * s + 1, unit, 0)
        return 0

    lax.fori_loop(0, 4, stage, 0)

    is_cond = c == 0
    width = pos_ref.shape[1]
    patch = wpatch_ref[...].astype(f32)
    patch = jnp.where(is_cond, patch[:, 0:width], patch[:, width : 2 * width]).astype(bf16)
    t_now = time_ref[0]
    sigma_now = sigma_ref[t_now].astype(f32) / 1000.0
    sigma_next = sigma_ref[t_now + 1].astype(f32) / 1000.0

    def collect(t):
        low = low_lanes(FIRST)
        for k in range(2):
            for dz in range(4):
                if t + k + dz == 0:
                    own_back.wait()
                else:
                    back_landed(t, k, dz).wait_recv()
            j, l = sender(t, k)
            n = j * 2 + l
            for pair in range(2):
                even = got[n, 2 * pair].astype(f32)
                odd = got[n, 2 * pair + 1].astype(f32)
                columns = pl.ds(pair * 128, 128)
                att[n, 0:FIRST, columns] = jnp.where(low, even, pltpu.roll(odd, HEAD, 1)).astype(bf16)
                rest = jnp.where(low, pltpu.roll(even, HEAD, 1), odd).astype(bf16)
                att[n, FIRST:ROWS, columns] = rest[2 * FIRST - ROWS : FIRST]

    def weights_there(t):
        for dx, dl in STAGES[t]:
            i = (4 - dx) % 4
            if dl == 1:
                out_core(i, True, True).wait_recv()
            elif i > 0:
                out_core(i, False, True).wait_recv()
            else:
                for copy in out_in:
                    copy.wait()

    def partial(t):
        total = 0.0
        for k in range(2):
            j, l = sender(t, k)
            weights = wo[j, l].reshape(2 * OUT_HALF, wo.shape[4])
            total += jnp.dot(att[j * 2 + l], weights, preferred_element_type=f32)
        return total

    pass_out(2)
    for t in range(3):
        collect(t)
        weights_there(t)
    projected = partial(0) + partial(1) + partial(2)
    collect(3)
    weights_there(3)
    projected = projected + partial(3)
    mixed = hid_ref[0].astype(f32) + mod_ref[2] * projected
    final = (layer_norm(mixed) * (1.0 + mod_ref[4]) + mod_ref[3]).astype(bf16)
    velocity = lax.dot_general(
        wfinal_ref[...], final, (((1,), (1,)), ((), ())), preferred_element_type=f32
    )
    vel[0] = velocity
    exchange = remote(vel.at[0], vel.at[1], vsend.at[0], vrecv.at[0], other)
    exchange.start()

    for i in range(9):
        sends[i].wait_send()
    for d in (1, 2, 3):
        text_z(d).wait_send()
        if d != 2:
            out_x(d).wait_send()
        out_core(d, False).wait_send()
    for k in (0, 1):
        out_x_on(k).wait_send()
    for d in range(4):
        for e in (1, 2, 3):
            text_y(d, e).wait_send()
        for copy in out_z(d):
            copy.wait_send()
        out_core(d, True).wait_send()
    for t in range(4):
        for d in (1, 2, 3):
            copy_kv(t, d).wait_send()
            copy_q(t, d).wait_send()
        for d in range(4):
            for e in (1, 2, 3):
                copy_y(t, d, e).wait_send()
            for k in range(2):
                if t + k + d > 0:
                    back(t, k, d).wait_send()

    exchange.wait()
    others = vel[1]
    cond = jnp.where(is_cond, velocity, others)
    uncond = jnp.where(is_cond, others, velocity)
    guided = uncond + guidance * (cond - uncond)
    latent = lat_ref[...] + (sigma_next - sigma_now) * guided
    embedded = jnp.dot(latent.T.astype(bf16), patch, preferred_element_type=f32)
    next_ref[...] = (embedded + pos_ref[...].astype(f32)).astype(bf16)
    channels = guided_ref.shape[0]
    guided_ref[...] = jnp.where(is_cond, guided[0:channels], guided[channels:])
    latent_ref[...] = jnp.where(is_cond, latent[0:channels], latent[channels:])


def body(
    hidden, text_states, modulation, w_qkv, w_text, w_out, qk_gain, w_final, w_patch,
    position, latent, text_len, timestep, sigma_table,
):
    width = hidden.shape[2]
    channels = latent.shape[1] // 2
    vmem = pl.BlockSpec(memory_space=pltpu.VMEM)
    hbm = pl.BlockSpec(memory_space=pl.ANY)
    smem = pl.BlockSpec(memory_space=pltpu.SMEM)
    dma = pltpu.SemaphoreType.DMA
    guided, next_latent, next_hidden = pl.pallas_call(
        kernel,
        out_shape=[
            jax.ShapeDtypeStruct((channels, ROWS), f32),
            jax.ShapeDtypeStruct((channels, ROWS), f32),
            jax.ShapeDtypeStruct(position.shape, bf16),
        ],
        in_specs=[vmem, vmem, vmem, hbm, hbm, hbm, vmem, vmem, vmem, vmem, vmem, smem, smem, smem],
        out_specs=[vmem, vmem, vmem],
        scratch_shapes=[
            pltpu.VMEM((8, ROWS, width), bf16),
            pltpu.VMEM((3, width, 256), bf16),
            pltpu.VMEM((2, width, 256), bf16),
            pltpu.VMEM((TXT_PAD, width), bf16),
            pltpu.VMEM((4, 4, PAIR, 128), bf16),
            pltpu.VMEM((4, 4, ROWS, 128), bf16),
            pltpu.VMEM((4, TXT_PAD, 128), bf16),
            pltpu.VMEM((4, KEYS, 128), bf16),
            pltpu.VMEM((4, KEYS, 128), bf16),
            pltpu.VMEM((4, 4, ROWS, 128), bf16),
            pltpu.VMEM((4, QUERIES, 128), bf16),
            pltpu.VMEM((TXT_KEYS, 128), bf16),
            pltpu.VMEM((TXT_KEYS, 128), bf16),
            pltpu.VMEM((4, QUERIES, 128), f32),
            pltpu.VMEM((4, QUERIES, 128), f32),
            pltpu.VMEM((4, 8, FIRST, 128), bf16),
            pltpu.VMEM((8, 4, FIRST, 128), bf16),
            pltpu.VMEM((8, ROWS, 2 * OUT_HALF), bf16),
            pltpu.VMEM((4, 2, 2, OUT_HALF, width), bf16),
            pltpu.VMEM((2, 2 * channels, ROWS), f32),
            dma((7,)), dma((10,)),
            dma((9,)), dma((9,)),
            dma((4, 3)), dma((4, 3)),
            dma((4, 3)), dma((4, 3)),
            dma((4, 4, 3)), dma((4, 4, 3)),
            dma((3,)), dma((3,)),
            dma((4, 3)), dma((4, 3)),
            dma((4,)), dma((4,)),
            dma((4,)), dma((4,)), dma((4,)), dma((4,)),
            dma((4,)), dma((4,)), dma((4,)), dma((4,)),
            dma((4, 2, 4)), dma((4, 2, 4)),
            dma((1,)), dma((1,)),
        ],
        compiler_params=pltpu.CompilerParams(
            collective_id=0, has_side_effects=True, vmem_limit_bytes=60 << 20
        ),
        name="sublayer",
    )(
        hidden, text_states, jnp.swapaxes(modulation, 0, 1), w_qkv, w_text, w_out, qk_gain,
        w_final.T, w_patch, position, latent.T, text_len, timestep, sigma_table,
    )
    return guided.T, next_latent.T, next_hidden


def solution(mesh):
    in_specs = (
        P("cfg", ("blk", "uly"), None),
        P("cfg", "blk", None),
        P("cfg", None, None),
        P(None, None, "uly"),
        P(None, None, "uly"),
        P("uly", None),
        P(),
        P(),
        P(),
        P(("blk", "uly"), "cfg"),
        P(("blk", "uly"), None),
        P("cfg"),
        P(),
        P(),
    )
    out_specs = (P(("blk", "uly"), "cfg"), P(("blk", "uly"), "cfg"), P(("blk", "uly"), "cfg"))
    return jax.shard_map(body, mesh=mesh, in_specs=in_specs, out_specs=out_specs, check_vma=False)
```

```python
import jax
import jax.numpy as jnp
import numpy as np
from jax import lax
from jax.experimental import pallas as pl
from jax.experimental.pallas import tpu as pltpu
from jax.sharding import PartitionSpec as P

HEAD = 64
guidance = 3.5
epsilon = 1e-06
MESH = pl.DeviceIdType.MESH
bf16 = jnp.bfloat16
f32 = jnp.float32

ROWS = 80
PAIR = 160
TXT_ROWS = 21
TXT_PAD = 32
TXT_KEYS = 16 * TXT_PAD
KEYS = 16 * PAIR
QUERIES = 4 * PAIR
FIRST = 48
OUT_HALF = 128
STAGES = (((0, 0), (0, 1)), ((3, 0), (1, 0)), ((3, 1), (1, 1)), ((2, 0), (2, 1)))


def layer_norm(values):
    average = jnp.mean(values, axis=-1, keepdims=True)
    centered = values - average
    spread = jnp.mean(centered * centered, axis=-1, keepdims=True)
    return centered * lax.rsqrt(spread + epsilon)


def low_lanes(rows):
    return lax.broadcasted_iota(jnp.int32, (rows, 128), 1) < HEAD


def head_norm(values, gain):
    low = low_lanes(values.shape[0])
    columns = []
    for t in range(2):
        x = values[:, 128 * t : 128 * t + 128]
        sq = x * x
        a = jnp.sum(jnp.where(low, sq, 0.0), axis=1, keepdims=True)
        b = jnp.sum(jnp.where(low, 0.0, sq), axis=1, keepdims=True)
        scale = lax.rsqrt(jnp.where(low, a, b) * (1.0 / HEAD) + epsilon)
        columns.append(x * scale * gain)
    return columns


def pack_heads(left, right):
    low = low_lanes(left[0].shape[0])
    out = []
    for t in range(2):
        out.append(jnp.where(low, left[t], pltpu.roll(right[t], HEAD, 1)))
        out.append(jnp.where(low, pltpu.roll(left[t], HEAD, 1), right[t]))
    return out


def values_and_ones(block):
    wide = block.astype(f32)
    return jnp.where(low_lanes(wide.shape[0]), pltpu.roll(wide, HEAD, 1), 1.0).astype(bf16)


def kernel(
    hid_ref, txt_ref, mod_ref, wqkv_ref, wtext_ref, wout_ref, gain_ref, wfinal_ref, wpatch_ref,
    pos_ref, lat_ref, len_ref, time_ref, sigma_ref,
    both_ref, next_ref,
    mods, wq, wt, txt, kvst, qst, tst, kvb, v1, qb, q2, tkv, tv1, top, acc, ob, got, att, wo, vel,
    wsem, lsem, bsend, brecv, zsend, zrecv, qsend, qrecv, ysend, yrecv,
    tzsend, tzrecv, tysend, tyrecv, xsend, xrecv, usend, urecv, dsend, drecv,
    csend, crecv, fsend, frecv, osend, orecv, vsend, vrecv,
):
    c = lax.axis_index("cfg")
    b = lax.axis_index("blk")
    u = lax.axis_index("uly")
    zh, y, x, zl = b // 4, b % 4, u // 2, u % 2

    def at(dz=0, dy=0, dx=0, dl=0):
        return (
            c,
            lax.rem(zh + dz, 4) * 4 + lax.rem(y + dy, 4),
            lax.rem(x + dx, 4) * 2 + lax.rem(zl + dl, 2),
        )

    other = (1 - c, b, u)
    partner, up, down = at(dl=1), at(dx=1), at(dx=3)
    above = (c, lax.rem(zh + zl, 4) * 4 + y, x * 2 + 1 - zl)
    below = (c, lax.rem(zh + 3 + zl, 4) * 4 + y, x * 2 + 1 - zl)
    far = (c, lax.rem(zh + 3 + 2 * zl, 4) * 4 + y, x * 2 + 1 - zl)

    qkv_in = [pltpu.make_async_copy(wqkv_ref.at[i], wq.at[i], wsem.at[i]) for i in range(3)]
    text_in = [pltpu.make_async_copy(wtext_ref.at[i], wt.at[i], wsem.at[3 + i]) for i in range(2)]
    out_in = [
        pltpu.make_async_copy(
            wout_ref.at[pl.ds(OUT_HALF * i, OUT_HALF)], wo.at[x, zl, i], wsem.at[5 + i]
        )
        for i in range(2)
    ]
    for copy in text_in + qkv_in + out_in:
        copy.start()

    barrier = pltpu.get_barrier_semaphore()
    peers = [at(dz=k // 8, dx=k % 8 // 2, dl=k % 2) for k in range(1, 32)]
    peers += [at(dy=d) for d in (1, 2, 3)] + [other]
    for peer in peers:
        pl.semaphore_signal(barrier, inc=1, device_id=peer, device_id_type=MESH)

    modulated = layer_norm(hid_ref[0].astype(f32)) * (1.0 + mod_ref[1]) + mod_ref[0]
    mods[u] = modulated.astype(bf16)
    txt[...] = jnp.zeros_like(txt)
    txt[0:TXT_ROWS, :] = txt_ref[0]
    pl.semaphore_wait(barrier, len(peers))

    def remote(src, dst, send, recv, to):
        return pltpu.make_async_remote_copy(
            src_ref=src, dst_ref=dst, send_sem=send, recv_sem=recv,
            device_id=to, device_id_type=MESH,
        )


    def shard(i, dx, dl, part, to):
        s = lax.rem(x + dx, 4) * 2 + (zl if dl == 0 else 1 - zl)
        ref = mods.at[s]
        if part == 1:
            ref = mods.at[s, pl.ds(0, FIRST)]
        elif part == 2:
            ref = mods.at[s, pl.ds(FIRST, ROWS - FIRST)]
        return remote(ref, ref, bsend.at[i], brecv.at[i], to)

    sends = [
        shard(0, 0, 0, 0, partner),
        shard(1, 0, 0, 0, up),
        shard(2, 0, 0, 0, down),
        shard(3, 0, 1, 0, up),
        shard(4, 0, 1, 0, down),
        shard(5, 3, 0, 1, up),
        shard(6, 1, 0, 2, down),
        shard(7, 3, 1, 1, up),
        shard(8, 1, 1, 2, down),
    ]
    arrive = [
        shard(0, 0, 1, 0, partner),
        shard(1, 3, 0, 0, up),
        shard(2, 1, 0, 0, down),
        shard(3, 3, 1, 0, up),
        shard(4, 1, 1, 0, down),
        shard(5, 2, 0, 1, up),
        shard(6, 2, 0, 2, down),
        shard(7, 2, 1, 1, up),
        shard(8, 2, 1, 2, down),
    ]
    for i in (0, 1, 2):
        sends[i].start()

    gain_q = gain_ref[0:1, :] * float(np.log2(np.e) * HEAD ** -0.5)
    gain_k = gain_ref[1:2, :]
    gain_q = jnp.concatenate([gain_q, gain_q], axis=1)
    gain_k = jnp.concatenate([gain_k, gain_k], axis=1)


    def source(d):
        return lax.rem(zh + 4 - d, 4) * 4 + y

    def kv_slot(t, block):
        return kvb.at[t, pl.ds(pl.multiple_of(block * PAIR, PAIR), PAIR)]

    def copy_kv(t, d):
        h = lax.rem(zh + d, 4)
        return remote(kvst.at[t, h], kv_slot(t, b), zsend.at[t, d - 1], zrecv.at[t, d - 1], at(dz=d))

    def landed_kv(t, d):
        slot = kv_slot(t, source(d))
        return remote(slot, slot, zsend.at[t, d - 1], zrecv.at[t, d - 1], at(dz=d))

    def copy_q(t, d):
        h = lax.rem(zh + d, 4)
        return remote(qst.at[t, h], qb.at[t, zh], qsend.at[t, d - 1], qrecv.at[t, d - 1], at(dz=d))

    def landed_q(t, d):
        slot = qb.at[t, lax.rem(zh + 4 - d, 4)]
        return remote(slot, slot, qsend.at[t, d - 1], qrecv.at[t, d - 1], at(dz=d))

    def copy_y(t, d, e):
        src = kvst.at[t, zh] if d == 0 else kv_slot(t, source(d))
        dst = kv_slot(t, source(d))
        return remote(src, dst, ysend.at[t, d, e - 1], yrecv.at[t, d, e - 1], at(dy=e))

    def landed_y(t, d, e):
        slot = kv_slot(t, lax.rem(zh + 4 - d, 4) * 4 + lax.rem(y + 4 - e, 4))
        return remote(slot, slot, ysend.at[t, d, e - 1], yrecv.at[t, d, e - 1], at(dy=e))

    def own_kv(t):
        return pltpu.make_async_copy(kvst.at[t, zh], kv_slot(t, b), lsem.at[t])

    def own_q(t):
        return pltpu.make_async_copy(qst.at[t, zh], qb.at[t, zh], lsem.at[4 + t])

    def text_slot(block):
        return tkv.at[pl.ds(pl.multiple_of(block * TXT_PAD, TXT_PAD), TXT_PAD)]

    def text_z(d):
        h = lax.rem(zh + d, 4)
        return remote(tst.at[h], text_slot(b), tzsend.at[d - 1], tzrecv.at[d - 1], at(dz=d))

    def text_z_landed(d):
        slot = text_slot(source(d))
        return remote(slot, slot, tzsend.at[d - 1], tzrecv.at[d - 1], at(dz=d))

    def text_y(d, e):
        src = tst.at[zh] if d == 0 else text_slot(source(d))
        return remote(src, text_slot(source(d)), tysend.at[d, e - 1], tyrecv.at[d, e - 1], at(dy=e))

    def text_y_landed(d, e):
        slot = text_slot(lax.rem(zh + 4 - d, 4) * 4 + lax.rem(y + 4 - e, 4))
        return remote(slot, slot, tysend.at[d, e - 1], tyrecv.at[d, e - 1], at(dy=e))

    own_text = pltpu.make_async_copy(tst.at[zh], text_slot(b), lsem.at[8])


    def out_x(d):
        src = wout_ref.at[pl.ds(pl.multiple_of(c * OUT_HALF, OUT_HALF), OUT_HALF)]
        return remote(src, wo.at[x, zl, c], xsend.at[d - 1], xrecv.at[d - 1], at(dx=d))

    def out_x_landed(d):
        slot = wo.at[lax.rem(x + 4 - d, 4), zl, c]
        return remote(slot, slot, xsend.at[d - 1], xrecv.at[d - 1], at(dx=d))

    half = OUT_HALF // 2

    def out_x_on(k):
        dx, to = ((3, up), (1, down))[k]
        ref = wo.at[lax.rem(x + dx, 4), zl, c, pl.ds(half * k, half)]
        return remote(ref, ref, xsend.at[1 + 2 * k], xrecv.at[1 + 2 * k], to)

    def out_x_on_landed(k):
        ref = wo.at[lax.rem(x + 2, 4), zl, c, pl.ds(half * k, half)]
        return remote(ref, ref, xsend.at[1 + 2 * k], xrecv.at[1 + 2 * k], (up, down)[k])

    def out_far():
        src = wout_ref.at[pl.ds(pl.multiple_of(c * OUT_HALF, OUT_HALF), OUT_HALF)]
        return remote(src, wo.at[x, zl, c], usend.at[0], urecv.at[0], far)

    def out_z(i):
        if i == 0:
            return [out_far()]
        j = lax.rem(x + i, 4)
        copies = []
        for k, to, send, recv in ((0, above, usend, urecv), (1, below, dsend, drecv)):
            ref = wo.at[j, zl, c, pl.ds(half * k, half)]
            copies.append(remote(ref, ref, send.at[i], recv.at[i], to))
        return copies

    def out_z_landed(i):
        j = lax.rem(x + i, 4)
        if i == 0:
            ref = wo.at[x, 1 - zl, c]
            return [remote(ref, ref, usend.at[0], urecv.at[0], far)]
        copies = []
        for k, to, send, recv in ((0, above, usend, urecv), (1, below, dsend, drecv)):
            ref = wo.at[j, 1 - zl, c, pl.ds(half * k, half)]
            copies.append(remote(ref, ref, send.at[i], recv.at[i], to))
        return copies

    def out_core(i, later, landed=False):
        j = lax.rem(x + i, 4)
        slot = wo.at[j, 1 - zl if later else zl, 1 - c if landed else c]
        send, recv = (fsend, frecv) if later else (csend, crecv)
        return remote(slot, slot, send.at[i], recv.at[i], other)

    def start_out_z(i):
        for copy in out_z(i):
            copy.start()

    def pass_out(i):
        for copy in out_z_landed(i):
            copy.wait_recv()
        out_core(i, True).start()


    def back(t, k, dz):
        dx, dl = STAGES[t][k]
        src = ob.at[t, lax.rem(zh + dz, 4) * 2 + k]
        return remote(src, got.at[u, zh], osend.at[t, k, dz], orecv.at[t, k, dz], at(dz=dz, dx=dx, dl=dl))

    def sender(t, k):
        dx, dl = STAGES[t][k]
        return lax.rem(x + 4 - dx, 4), lax.rem(zl + dl, 2)

    def back_landed(t, k, dz):
        dx, dl = STAGES[t][k]
        j, l = sender(t, k)
        slot = got.at[j * 2 + l, lax.rem(zh + 4 - dz, 4)]
        return remote(slot, slot, osend.at[t, k, dz], orecv.at[t, k, dz], at(dz=dz, dx=dx, dl=dl))

    own_back = pltpu.make_async_copy(ob.at[0, zh * 2], got.at[u, zh], lsem.at[9])

    for copy in text_in:
        copy.wait()
    rows = txt[...]
    tk = head_norm(jnp.dot(rows, wt[0], preferred_element_type=f32), gain_k)
    tv = jnp.dot(rows, wt[1], preferred_element_type=f32)
    for h, value in enumerate(pack_heads(tk, [tv[:, 0:128], tv[:, 128:256]])):
        tst[h] = value.astype(bf16)
    for d in (1, 2, 3):
        text_z(d).start()
    for e in (1, 2, 3):
        text_y(0, e).start()
    own_text.start()
    for copy in qkv_in:
        copy.wait()

    def project(t):
        pair = jnp.concatenate(
            [mods[lax.rem(x + dx, 4) * 2 + lax.rem(zl + dl, 2)] for dx, dl in STAGES[t]], axis=0
        )
        ks = head_norm(jnp.dot(pair, wq[1], preferred_element_type=f32), gain_k)
        vs = jnp.dot(pair, wq[2], preferred_element_type=f32)
        for h, value in enumerate(pack_heads(ks, [vs[:, 0:128], vs[:, 128:256]])):
            kvst[t, h] = value.astype(bf16)
        for d in (2, 1, 3):
            copy_kv(t, d).start()
        for e in (2, 1, 3):
            copy_y(t, 0, e).start()
        own_kv(t).start()
        qs = head_norm(jnp.dot(pair, wq[0], preferred_element_type=f32), gain_q)
        for h, value in enumerate(pack_heads([v[0:ROWS] for v in qs], [v[ROWS:PAIR] for v in qs])):
            qst[t, h] = value.astype(bf16)
        for d in (2, 1, 3):
            copy_q(t, d).start()
        own_q(t).start()

    def pass_on(t):
        for d in (1, 3, 2):
            landed_kv(t, d).wait_recv()
            for e in (2, 1, 3):
                copy_y(t, d, e).start()

    arrive[0].wait_recv()
    sends[3].start()
    sends[4].start()
    arrive[1].wait_recv()
    sends[5].start()
    arrive[2].wait_recv()
    sends[6].start()
    project(0)
    project(1)
    for d in (1, 2, 3):
        text_z_landed(d).wait_recv()
        for e in (1, 2, 3):
            text_y(d, e).start()
    pass_on(0)
    arrive[3].wait_recv()
    sends[7].start()
    arrive[4].wait_recv()
    sends[8].start()
    project(2)
    pass_on(1)
    own_text.wait()
    for d in range(4):
        for e in (1, 2, 3):
            text_y_landed(d, e).wait_recv()
    tv1[...] = values_and_ones(tkv[...])

    def fold(carry, q, keys, values, usable):
        high, total = carry
        scores = lax.dot_general(q, keys, (((1,), (1,)), ((), ())), preferred_element_type=f32)
        if usable is not None:
            scores = jnp.where(usable, scores, -1e30)
        new_high = jnp.maximum(high, jnp.max(scores, axis=1, keepdims=True))
        wide = jnp.concatenate([new_high] * (keys.shape[0] // 128), axis=1)
        weights = jnp.exp2(scores - wide).astype(bf16)
        shrink = jnp.exp2(high - new_high)
        return new_high, total * shrink + jnp.dot(weights, values, preferred_element_type=f32)

    row = lax.broadcasted_iota(jnp.int32, (1, TXT_KEYS), 1)
    block = row // TXT_PAD
    within = row - block * TXT_PAD
    usable = jnp.logical_and(within < TXT_ROWS, block * TXT_ROWS + within < len_ref[0])

    def stage(s, _):
        @pl.when(s == 1)
        def _():
            for i in (5, 6, 7, 8):
                arrive[i].wait_recv()
            out_x(1).start()
            out_x(3).start()
            project(3)
            pass_on(2)

        own_q(s).wait()
        for d in (1, 2, 3):
            landed_q(s, d).wait_recv()
        low = low_lanes(ROWS)
        for p in range(4):
            packed = qb[s, p].astype(f32)
            q2[s, PAIR * p : PAIR * p + ROWS, :] = jnp.where(low, packed, 0.0).astype(bf16)
            q2[s, PAIR * p + ROWS : PAIR * p + PAIR, :] = jnp.where(
                low, pltpu.roll(packed, HEAD, 1), 0.0
            ).astype(bf16)
        first = (jnp.full((QUERIES, 128), -1e30, f32), jnp.zeros((QUERIES, 128), f32))
        top[s], acc[s] = fold(first, q2[s], tkv[...], tv1[...], usable)
        own_kv(s).wait()
        for d in range(4):
            for e in (1, 2, 3):
                landed_y(s, d, e).wait_recv()

        @pl.loop(0, KEYS // 512)
        def _(n):
            rows = pl.ds(pl.multiple_of(n * 512, 512), 512)
            v1[s, rows] = values_and_ones(kvb[s, rows])

        def unit(j, _):
            i = jnp.minimum(j, s)
            k = jnp.where(j < s, s, j - s)
            high, total = fold((top[i], acc[i]), q2[i], kvb[k], v1[k], None)
            top[i] = high
            acc[i] = total

            @pl.when(jnp.logical_and(s == 1, j == 1))
            def _():
                pass_on(3)
                out_far().start()

            @pl.when(jnp.logical_and(s == 2, j == 2))
            def _():
                for i in (1, 3):
                    out_x_landed(i).wait_recv()
                for k in (0, 1):
                    out_x_on(k).start()
                for i in (1, 3):
                    start_out_z(i)
                    out_core(i, False).start()

            @pl.when(jnp.logical_and(s == 3, j == 0))
            def _():
                pass_out(0)
                for k in (0, 1):
                    out_x_on_landed(k).wait_recv()
                    out_z(2)[k].start()
                out_core(2, False).start()

            @pl.when(jnp.logical_and(s == 3, j == 3))
            def _():
                pass_out(1)

            @pl.when(jnp.logical_and(s == 3, j == 4))
            def _():
                pass_out(3)

            @pl.when(jnp.logical_and(s == 3, jnp.logical_or(j < 3, j == 6)))
            def _():
                out = acc[i]
                out = out / out[:, HEAD : HEAD + 1]
                turned = pltpu.roll(out, HEAD, 1)
                low = low_lanes(FIRST)
                for n in range(8):
                    ob[i, n] = jnp.where(
                        low,
                        out[ROWS * n : ROWS * n + FIRST],
                        turned[ROWS * (n + 1) - FIRST : ROWS * (n + 1)],
                    ).astype(bf16)
                for t in range(4):

                    @pl.when(i == t)
                    def _():
                        for dz in (2, 1, 3, 0):
                            for k in range(2):
                                if t + k + dz == 0:
                                    own_back.start()
                                else:
                                    back(t, k, dz).start()

            return 0

        lax.fori_loop(0, 2 * s + 1, unit, 0)
        return 0

    lax.fori_loop(0, 4, stage, 0)

    is_cond = c == 0
    width = pos_ref.shape[1]
    patch = wpatch_ref[...].astype(f32)
    patch = jnp.where(is_cond, patch[:, 0:width], patch[:, width : 2 * width]).astype(bf16)
    t_now = time_ref[0]
    sigma_now = sigma_ref[t_now].astype(f32) / 1000.0
    sigma_next = sigma_ref[t_now + 1].astype(f32) / 1000.0

    def collect(t):
        low = low_lanes(FIRST)
        for k in range(2):
            for dz in range(4):
                if t + k + dz == 0:
                    own_back.wait()
                else:
                    back_landed(t, k, dz).wait_recv()
            j, l = sender(t, k)
            n = j * 2 + l
            for pair in range(2):
                even = got[n, 2 * pair].astype(f32)
                odd = got[n, 2 * pair + 1].astype(f32)
                columns = pl.ds(pair * 128, 128)
                att[n, 0:FIRST, columns] = jnp.where(low, even, pltpu.roll(odd, HEAD, 1)).astype(bf16)
                rest = jnp.where(low, pltpu.roll(even, HEAD, 1), odd).astype(bf16)
                att[n, FIRST:ROWS, columns] = rest[2 * FIRST - ROWS : FIRST]

    def weights_there(t):
        for dx, dl in STAGES[t]:
            i = (4 - dx) % 4
            if dl == 1:
                out_core(i, True, True).wait_recv()
            elif i > 0:
                out_core(i, False, True).wait_recv()
            else:
                for copy in out_in:
                    copy.wait()

    def partial(t):
        total = 0.0
        for k in range(2):
            j, l = sender(t, k)
            weights = wo[j, l].reshape(2 * OUT_HALF, wo.shape[4])
            total += jnp.dot(att[j * 2 + l], weights, preferred_element_type=f32)
        return total

    collect(0)
    weights_there(0)
    projected = partial(0)
    pass_out(2)
    for t in (1, 2):
        collect(t)
        weights_there(t)
    projected = projected + partial(1) + partial(2)
    collect(3)
    weights_there(3)
    projected = projected + partial(3)
    mixed = hid_ref[0].astype(f32) + mod_ref[2] * projected
    final = (layer_norm(mixed) * (1.0 + mod_ref[4]) + mod_ref[3]).astype(bf16)
    velocity = lax.dot_general(
        wfinal_ref[...], final, (((1,), (1,)), ((), ())), preferred_element_type=f32
    )
    vel[0] = velocity
    exchange = remote(vel.at[0], vel.at[1], vsend.at[0], vrecv.at[0], other)
    exchange.start()

    for i in range(9):
        sends[i].wait_send()
    for d in (1, 2, 3):
        text_z(d).wait_send()
        if d != 2:
            out_x(d).wait_send()
        out_core(d, False).wait_send()
    for k in (0, 1):
        out_x_on(k).wait_send()
    for d in range(4):
        for e in (1, 2, 3):
            text_y(d, e).wait_send()
        for copy in out_z(d):
            copy.wait_send()
        out_core(d, True).wait_send()
    for t in range(4):
        for d in (1, 2, 3):
            copy_kv(t, d).wait_send()
            copy_q(t, d).wait_send()
        for d in range(4):
            for e in (1, 2, 3):
                copy_y(t, d, e).wait_send()
            for k in range(2):
                if t + k + d > 0:
                    back(t, k, d).wait_send()

    exchange.wait()
    others = vel[1]
    cond = jnp.where(is_cond, velocity, others)
    uncond = jnp.where(is_cond, others, velocity)
    guided = uncond + guidance * (cond - uncond)
    latent = lat_ref[...] + (sigma_next - sigma_now) * guided
    embedded = jnp.dot(latent.T.astype(bf16), patch, preferred_element_type=f32)
    next_ref[...] = (embedded + pos_ref[...].astype(f32)).astype(bf16)
    channels = both_ref.shape[1]
    both_ref[0] = jnp.where(is_cond, guided[0:channels], guided[channels:])
    both_ref[1] = jnp.where(is_cond, latent[0:channels], latent[channels:])


def body(
    hidden, text_states, modulation, w_qkv, w_text, w_out, qk_gain, w_final, w_patch,
    position, latent, text_len, timestep, sigma_table,
):
    width = hidden.shape[2]
    channels = latent.shape[1] // 2
    vmem = pl.BlockSpec(memory_space=pltpu.VMEM)
    hbm = pl.BlockSpec(memory_space=pl.ANY)
    smem = pl.BlockSpec(memory_space=pltpu.SMEM)
    dma = pltpu.SemaphoreType.DMA
    both, next_hidden = pl.pallas_call(
        kernel,
        out_shape=[
            jax.ShapeDtypeStruct((2, channels, ROWS), f32),
            jax.ShapeDtypeStruct(position.shape, bf16),
        ],
        in_specs=[vmem, vmem, vmem, hbm, hbm, hbm, vmem, vmem, vmem, vmem, vmem, smem, smem, smem],
        out_specs=[vmem, vmem],
        scratch_shapes=[
            pltpu.VMEM((8, ROWS, width), bf16),
            pltpu.VMEM((3, width, 256), bf16),
            pltpu.VMEM((2, width, 256), bf16),
            pltpu.VMEM((TXT_PAD, width), bf16),
            pltpu.VMEM((4, 4, PAIR, 128), bf16),
            pltpu.VMEM((4, 4, ROWS, 128), bf16),
            pltpu.VMEM((4, TXT_PAD, 128), bf16),
            pltpu.VMEM((4, KEYS, 128), bf16),
            pltpu.VMEM((4, KEYS, 128), bf16),
            pltpu.VMEM((4, 4, ROWS, 128), bf16),
            pltpu.VMEM((4, QUERIES, 128), bf16),
            pltpu.VMEM((TXT_KEYS, 128), bf16),
            pltpu.VMEM((TXT_KEYS, 128), bf16),
            pltpu.VMEM((4, QUERIES, 128), f32),
            pltpu.VMEM((4, QUERIES, 128), f32),
            pltpu.VMEM((4, 8, FIRST, 128), bf16),
            pltpu.VMEM((8, 4, FIRST, 128), bf16),
            pltpu.VMEM((8, ROWS, 2 * OUT_HALF), bf16),
            pltpu.VMEM((4, 2, 2, OUT_HALF, width), bf16),
            pltpu.VMEM((2, 2 * channels, ROWS), f32),
            dma((7,)), dma((10,)),
            dma((9,)), dma((9,)),
            dma((4, 3)), dma((4, 3)),
            dma((4, 3)), dma((4, 3)),
            dma((4, 4, 3)), dma((4, 4, 3)),
            dma((3,)), dma((3,)),
            dma((4, 3)), dma((4, 3)),
            dma((4,)), dma((4,)),
            dma((4,)), dma((4,)), dma((4,)), dma((4,)),
            dma((4,)), dma((4,)), dma((4,)), dma((4,)),
            dma((4, 2, 4)), dma((4, 2, 4)),
            dma((1,)), dma((1,)),
        ],
        compiler_params=pltpu.CompilerParams(
            collective_id=0, has_side_effects=True, vmem_limit_bytes=60 << 20
        ),
        name="sublayer",
    )(
        hidden, text_states, jnp.swapaxes(modulation, 0, 1), w_qkv, w_text, w_out, qk_gain,
        w_final.T, w_patch, position, latent.T, text_len, timestep, sigma_table,
    )
    return both[0].T, both[1].T, next_hidden


def solution(mesh):
    in_specs = (
        P("cfg", ("blk", "uly"), None),
        P("cfg", "blk", None),
        P("cfg", None, None),
        P(None, None, "uly"),
        P(None, None, "uly"),
        P("uly", None),
        P(),
        P(),
        P(),
        P(("blk", "uly"), "cfg"),
        P(("blk", "uly"), None),
        P("cfg"),
        P(),
        P(),
    )
    out_specs = (P(("blk", "uly"), "cfg"), P(("blk", "uly"), "cfg"), P(("blk", "uly"), "cfg"))
    return jax.shard_map(body, mesh=mesh, in_specs=in_specs, out_specs=out_specs, check_vma=False)
```
